512 devices in a mesh: recv: 64 (over z, y_hi, core), win: 8 (over x, y_lo).
Axes of the slice: x: 4, y: 8 (y_hi: 4, y_lo: 2; y = y_hi * 2 + y_lo), z: 8, core: 2. Of those that a mesh axis runs over, the one named last changes fastest.
Arguments:
- spectra: float32 [8, 256, 2, 4352], P('win', 'recv'), may hold values from -6 to 6
- sources: int32 [16], replicated, may hold values from 0 to 255
Outputs:
- correlograms: float32 [16, 256, 1001], P('win', 'recv')
The draws below stay inside these ranges and needn't reach their ends.
All inputs are finite; a program needn't handle non-finite values.
Results may differ from the reference program's by a relative error of at most 0.0001.
Values sent between devices are 32-bit elements; how exact they have to be, the bound alone decides.
A program may use at most 64 MiB of HBM per device.

```python
import math
import jax
import jax.numpy as jnp
from jax import lax

BINS = 4352
NFFT = 16384
FIRST = 256
HALF = 500
NSRC = 16
CHANNELS = 256
WINDOWS = 8


def with_ends(values, stream_key, smallest, high):
    extent = values.shape
    index_at = [jax.random.randint(jax.random.fold_in(stream_key, axis), (), 0, extent[axis]) for axis in range(len(extent))]
    values = values.at[tuple(index_at)].set(smallest)
    longest = extent.index(max(extent))
    index_at[longest] = (index_at[longest] + 1) % extent[longest]
    return values.at[tuple(index_at)].set(high)


def shard_levels(rng, dims, split, low, high):
    def one(position, blocks):
        steps = jax.random.uniform(jax.random.fold_in(jax.random.fold_in(rng, 6), position), (blocks,), jnp.float32, low / len(split), high / len(split))
        return jnp.repeat(jnp.exp(steps), dims[position] // blocks).reshape((-1,) + (1,) * (len(dims) - position - 1))

    level = one(*split[0])
    for cut in split[1:]:
        level = level * one(*cut)
    return level


def normal_values(key, dims, scale, bound, shards=(), held_as=jnp.bfloat16):
    values = scale * jax.random.normal(key, dims, jnp.float32)
    if shards:
        values = values * shard_levels(key, dims, shards, -0.22, 0.18)
    return jnp.clip(values, -bound, bound).astype(held_as)


def setup_inputs(seed: int = 0) -> dict:
    seeds = jax.random.split(jax.random.key(seed), 3)
    spectra = normal_values(seeds[0], (WINDOWS, CHANNELS, 2, BINS), 1.0, 6.0, ((0, 8), (1, 64)), jnp.float32)
    sources = with_ends(jax.random.randint(seeds[1], (NSRC,), 0, CHANNELS), jax.random.fold_in(seeds[1], 1), 0, CHANNELS - 1).astype(jnp.int32)
    return dict(spectra=spectra, sources=sources)


def whiten(spectra):
    power = lax.optimization_barrier(jnp.sum(spectra * spectra, axis=(-2, -1), keepdims=True)) / spectra.shape[-1]
    return spectra * lax.rsqrt(power + 1e-06)

def lag_table(start, width, windows):
    freqs = FIRST + start + jnp.arange(width, dtype=jnp.int32)
    shifts = jnp.arange(2 * HALF + 1, dtype=jnp.int32) - HALF
    phase = (freqs[:, None] * shifts[None, :] % NFFT).astype(jnp.float32) * (2.0 * math.pi / NFFT)
    bins_at = (start + jnp.arange(width, dtype=jnp.int32)).astype(jnp.float32)
    taper = jnp.sin(math.pi * (bins_at + 0.5) / BINS) / jnp.sqrt(jnp.float32(windows * BINS))
    return (jnp.cos(phase) * taper[:, None], -jnp.sin(phase) * taper[:, None])

def inverse_lags(real_part, imag_part, windows):
    lead = real_part.shape[:-1]
    nbins = real_part.shape[-1]
    real_rows = real_part.reshape(-1, nbins)
    imag_rows = imag_part.reshape(-1, nbins)
    width = math.gcd(nbins, 256)

    def step(index, total):
        start = (index * width).astype(jnp.int32)
        cosines, sines = lag_table(start, width, windows)
        left = lax.dynamic_slice_in_dim(real_rows, start, width, 1)
        right = lax.dynamic_slice_in_dim(imag_rows, start, width, 1)
        total = total + jnp.dot(left, cosines, precision=lax.Precision.HIGHEST)
        return total + jnp.dot(right, sines, precision=lax.Precision.HIGHEST)
    empty = jnp.zeros((real_rows.shape[0], 2 * HALF + 1), jnp.float32)
    total = lax.fori_loop(0, nbins // width, step, empty)
    return total.reshape(lead + (2 * HALF + 1,))

def reference(spectra, sources):
    white = whiten(spectra)
    source = white[:, sources]
    high = lax.Precision.HIGHEST
    cross_re = jnp.einsum('wkb,wcb->kcb', source[:, :, 0], white[:, :, 0], precision=high)
    cross_re = cross_re + jnp.einsum('wkb,wcb->kcb', source[:, :, 1], white[:, :, 1], precision=high)
    cross_im = jnp.einsum('wkb,wcb->kcb', source[:, :, 1], white[:, :, 0], precision=high)
    cross_im = cross_im - jnp.einsum('wkb,wcb->kcb', source[:, :, 0], white[:, :, 1], precision=high)
    return inverse_lags(cross_re, cross_im, WINDOWS)
```

```python
import math

import jax
import jax.numpy as jnp
import numpy as np
from jax import lax
from jax.experimental import pallas as pl
from jax.experimental.pallas import tpu as pltpu
from jax.sharding import PartitionSpec as P

BINS = 4352
NFFT = 16384
FIRST = 256
HALF = 500
LAGS = 2 * HALF + 1
NSRC = 16
WINDOWS = 8
CHAN = 4
DEPTH = 8
ROWS = 4
RECV = 64
TILES = BINS // 128
OWN = 4
LEFT = TILES - OWN * WINDOWS
WORK = OWN + LEFT
WIDE = 1024
CUT = 256
CUTS = WIDE // CUT
ITEMS = WINDOWS * OWN + LEFT
MESH = pl.DeviceIdType.MESH
F32 = jnp.float32
BF16 = jnp.bfloat16


def tables():
    lags = np.arange(WIDE, dtype=np.int64) - HALF
    turn = 2.0 * np.pi / NFFT
    inner = (np.arange(128)[:, None] * lags[None, :]) % NFFT * turn
    base = np.concatenate([np.cos(inner), np.sin(inner)]).astype(np.float32)
    first = FIRST + 128 * np.arange(TILES, dtype=np.int64)
    outer = (first[:, None] * lags[None, :]) % NFFT * turn
    rot = np.zeros((TILES, 8, WIDE), np.float32)
    rot[:, 0] = np.cos(outer)
    rot[:, 1] = np.sin(outer)
    taper = np.sin(np.pi * (np.arange(BINS) + 0.5) / BINS) / math.sqrt(WINDOWS * BINS)
    rot[:, 2, :128] = taper.reshape(TILES, 128)
    return base, rot


def kernel(
    spec_hbm, src, base_hbm, rot_hbm, out,
    spec, white, heard, chans, items, base, rot, thi, tlo, cross, part, parts,
    load_sem, own_sem, hear_send, hear_recv, chan_send, chan_recv, item_send, item_recv, part_send, part_recv,
):
    r = lax.axis_index("recv")
    w = lax.axis_index("win")
    core = lax.rem(r, 2)
    y = lax.rem(lax.div(r, 2), ROWS)
    z = lax.div(r, 2 * ROWS)

    def at(z2, y2, core2):
        return (z2 * ROWS + y2) * 2 + core2

    regular = core == lax.rem(y, 2)
    left = (z == w) & (((y == 0) & (core == 1)) | ((y == 1) & (core == 0)))
    holder = regular | left
    mine = jnp.where(regular, z * OWN + y, WINDOWS * OWN + jnp.where(core == 0, 1, 0))

    loads = [
        pltpu.make_async_copy(spec_hbm, spec, load_sem.at[0]),
        pltpu.make_async_copy(base_hbm, base, load_sem.at[1]),
        pltpu.make_async_copy(rot_hbm.at[pl.ds(OWN * w, OWN)], rot.at[pl.ds(0, OWN)], load_sem.at[2]),
        pltpu.make_async_copy(rot_hbm.at[pl.ds(OWN * WINDOWS, LEFT)], rot.at[pl.ds(OWN, LEFT)], load_sem.at[3]),
    ]
    for load in loads:
        load.start()

    barrier = pltpu.get_barrier_semaphore()

    def greet(r2, w2):
        pl.semaphore_signal(barrier, inc=1, device_id=(r2, w2), device_id_type=MESH)

    @pl.when(holder)
    def _():
        def one(r2, carry):
            @pl.when((r2 != r) | (z != w))
            def _():
                greet(r2, z)

            return carry

        lax.fori_loop(0, RECV, one, 0)

    def others(size, me):
        return [lax.rem(me + d, size) for d in range(1, size)]

    for w2 in others(WINDOWS, w):
        greet(r, w2)
    for z2 in others(DEPTH, z):
        greet(at(z2, y, core), w)
    for y2 in others(ROWS, y):
        greet(at(z, y2, core), w)
    greet(at(z, y, 1 - core), w)

    loads[0].wait()
    for c in range(CHAN):
        both = spec[0, c]
        power = jnp.sum(both * both, axis=(0, 1), keepdims=True) / BINS
        both = both * lax.rsqrt(power + 1e-06)
        for t in range(TILES):
            white[t, c : c + 1, :] = both[0:1, 128 * t : 128 * t + 128]
            white[t, CHAN + c : CHAN + c + 1, :] = both[1:2, 128 * t : 128 * t + 128]

    own_chans = pltpu.make_async_copy(white.at[pl.ds(OWN * w, OWN)], chans.at[w], own_sem.at[0])
    own_chans.start()

    self_held = holder & (z == w)
    pl.semaphore_wait(barrier, jnp.where(self_held, TILES - 1, TILES) + 7 + 7 + 3 + 1)

    def tell(i, carry):
        t = lax.rem(i + r, TILES)
        q = lax.rem(t, OWN)
        in_col = t < OWN * WINDOWS
        w2 = jnp.where(in_col, lax.div(t, OWN), w)
        r2 = jnp.where(in_col, at(w, q, lax.rem(q, 2)), jnp.where(t == OWN * WINDOWS, at(w, 0, 1), at(w, 1, 0)))
        self = (r2 == r) & (w2 == w)

        @pl.when(self)
        def _():
            pltpu.make_async_copy(white.at[t], heard.at[r], hear_recv).start()

        @pl.when(jnp.logical_not(self))
        def _():
            pltpu.make_async_remote_copy(
                white.at[t], heard.at[r], hear_send, hear_recv, device_id=(r2, w2), device_id_type=MESH
            ).start()

        return carry

    lax.fori_loop(0, TILES, tell, 0)
    for w2 in others(WINDOWS, w):
        pltpu.make_async_remote_copy(
            white.at[pl.ds(OWN * w2, OWN)], chans.at[w], chan_send, chan_recv, device_id=(r, w2), device_id_type=MESH
        ).start()

    for load in loads[1:]:
        load.wait()

    def table(i, carry):
        u = lax.div(i, 8)
        row = pl.multiple_of(lax.rem(i, 8) * 16, 16)
        ct = rot[u, 0:1, :]
        st = rot[u, 1:2, :]
        cb = base[pl.ds(row, 16), :]
        sb = base[pl.ds(row + 128, 16), :]
        at_re = pl.multiple_of(u * 256 + row, 16)
        for value, place in ((cb * ct - sb * st, at_re), (-(sb * ct + cb * st), at_re + 128)):
            high = value.astype(BF16)
            thi[pl.ds(place, 16), :] = high
            tlo[pl.ds(place, 16), :] = (value - high.astype(F32)).astype(BF16)
        return carry

    lax.fori_loop(0, WORK * 8, table, 0)

    def send_item(i, r2):
        pltpu.make_async_remote_copy(
            items.at[i], items.at[i], item_send.at[i], item_recv.at[i], device_id=(r2, w), device_id_type=MESH
        ).start()

    def await_item(i):
        pltpu.make_async_copy(items.at[i], items.at[i], item_recv.at[i]).wait()

    def to_core(i):
        send_item(i, at(z, y, 1 - core))

    def to_rows(i):
        for y2 in others(ROWS, y):
            send_item(i, at(z, y2, core))

    def to_depth(i):
        for z2 in others(DEPTH, z):
            send_item(i, at(z2, y, core))

    @pl.when(holder)
    def _():
        pltpu.make_async_copy(heard, heard, hear_recv).wait()
        for k in range(NSRC):
            s = src[k]
            d = lax.shift_right_logical(s, 2)
            c = lax.bitwise_and(s, 3)
            items[mine, k : k + 1, :] = heard[d, pl.ds(c, 1), :]
            items[mine, NSRC + k : NSRC + k + 1, :] = heard[d, pl.ds(c + CHAN, 1), :]

    spare = WINDOWS * OWN

    @pl.when(core == 0)
    def _():
        @pl.when(holder)
        def _():
            to_rows(mine)
            to_depth(mine)
            to_core(mine)

        for q in (0, 2):

            @pl.when(y != q)
            def _():
                await_item(z * OWN + q)
                to_depth(z * OWN + q)
                to_core(z * OWN + q)

        @pl.when((z == w) & (y != 1))
        def _():
            await_item(spare + 1)
            to_depth(spare + 1)
            to_core(spare + 1)

        for z2 in others(DEPTH, z):
            for q in (0, 2):
                await_item(z2 * OWN + q)
                to_core(z2 * OWN + q)

        @pl.when(z != w)
        def _():
            await_item(spare + 1)
            to_core(spare + 1)

        for z2 in range(DEPTH):
            for q in (1, 3):
                await_item(z2 * OWN + q)
        await_item(spare)

    @pl.when(core == 1)
    def _():
        @pl.when(holder)
        def _():
            to_depth(mine)
            to_rows(mine)
            to_core(mine)

        @pl.when(regular)
        def _():
            for z2 in others(DEPTH, z):
                await_item(z2 * OWN + y)
                to_rows(z2 * OWN + y)
                to_core(z2 * OWN + y)

        @pl.when((y == 0) & (z != w))
        def _():
            await_item(spare)
            to_rows(spare)
            to_core(spare)

        for q in (1, 3):

            @pl.when(y != q)
            def _():
                for z2 in range(DEPTH):
                    await_item(z2 * OWN + q)
                    to_core(z2 * OWN + q)

        @pl.when(y != 0)
        def _():
            await_item(spare)
            to_core(spare)

        for z2 in range(DEPTH):
            for q in (0, 2):
                await_item(z2 * OWN + q)
        await_item(spare + 1)

    own_chans.wait()
    for _w2 in range(1):
        pltpu.make_async_copy(chans.at[pl.ds(0, 7)], chans.at[pl.ds(0, 7)], chan_recv).wait()

    upper = lax.broadcasted_iota(jnp.int32, (8, 128), 0) < CHAN

    def add(total, chan, i):
        turned = pltpu.roll(chan, CHAN, 0)
        plus = jnp.where(upper, chan, -chan)
        return tuple(
            total[k] + items[i, k : k + 1, :] * plus + items[i, NSRC + k : NSRC + k + 1, :] * turned
            for k in range(NSRC)
        )

    def put(u, total):
        taper = rot[u, 2:3, 0:128]
        col = pl.multiple_of(u * 256, 256)
        for p in range(NSRC // 4):
            halves = []
            for g in (2 * p, 2 * p + 1):
                a, b = total[2 * g], total[2 * g + 1]
                re = jnp.where(upper, a, pltpu.roll(b, CHAN, 0)) * taper
                im = jnp.where(upper, pltpu.roll(a, CHAN, 0), b) * taper
                halves.append((re, im))
            for j in range(2):
                value = jnp.concatenate([halves[0][j], halves[1][j]], axis=0)
                high = value.astype(BF16)
                cross[16 * p : 16 * p + 16, pl.ds(col + 128 * j, 128)] = high
                cross[64 + 16 * p : 64 + 16 * p + 16, pl.ds(col + 128 * j, 128)] = (
                    value - high.astype(F32)
                ).astype(BF16)

    nothing = tuple(jnp.zeros((8, 128), F32) for _ in range(NSRC))

    def tile(q, carry):
        put(q, lax.fori_loop(0, WINDOWS, lambda v, total: add(total, chans[v, q], v * OWN + q), nothing))
        return carry

    lax.fori_loop(0, OWN, tile, 0)

    def tail(j, carry):
        put(OWN + j, add(nothing, white[spare + j], spare + j))
        return carry

    lax.fori_loop(0, LEFT, tail, 0)

    for n in range(CUTS):
        cols = slice(CUT * n, CUT * n + CUT)
        both = jnp.dot(cross[...], thi[:, cols], preferred_element_type=F32)
        low = jnp.dot(cross[0:64, :], tlo[:, cols], preferred_element_type=F32)
        value = both[0:64] + both[64:128] + low
        for g in range(WINDOWS):
            part[n * WINDOWS + g] = value[8 * g : 8 * g + 8]
        pltpu.make_async_copy(part.at[n * WINDOWS + w], parts.at[w, n], own_sem.at[1]).start()
        for w2 in others(WINDOWS, w):
            pltpu.make_async_remote_copy(
                part.at[n * WINDOWS + w2], parts.at[w, n], part_send, part_recv, device_id=(r, w2), device_id_type=MESH
            ).start()

    pltpu.make_async_copy(parts.at[0], parts.at[0], own_sem.at[1]).wait()
    pltpu.make_async_copy(parts.at[pl.ds(0, 7)], parts.at[pl.ds(0, 7)], part_recv).wait()
    for n in range(CUTS):
        width = min(CUT, LAGS - CUT * n)
        total = parts[0, n]
        for v in range(1, WINDOWS):
            total = total + parts[v, n]
        for k in range(2):
            out[k, :, CUT * n : CUT * n + width] = total[CHAN * k : CHAN * k + CHAN, 0:width]

    many = pl.ds(0, WORK + 1)
    pltpu.make_async_copy(chans.at[pl.ds(0, 7)], chans.at[pl.ds(0, 7)], chan_send).wait()
    pltpu.make_async_copy(part.at[pl.ds(0, 7 * CUTS)], part.at[pl.ds(0, 7 * CUTS)], part_send).wait()

    @pl.when(self_held)
    def _():
        pltpu.make_async_copy(white.at[pl.ds(0, TILES - 1)], white.at[pl.ds(0, TILES - 1)], hear_send).wait()

    @pl.when(jnp.logical_not(self_held))
    def _():
        pltpu.make_async_copy(white, white, hear_send).wait()

    def sent(i, count):
        pltpu.make_async_copy(items.at[pl.ds(0, count)], items.at[pl.ds(0, count)], item_send.at[i]).wait()

    @pl.when(holder)
    def _():
        sent(mine, 11)

    @pl.when(core == 0)
    def _():
        for q in (0, 2):

            @pl.when(y != q)
            def _():
                sent(z * OWN + q, 8)

        @pl.when((z == w) & (y != 1))
        def _():
            sent(spare + 1, 8)

        for z2 in others(DEPTH, z):
            for q in (0, 2):
                sent(z2 * OWN + q, 1)

        @pl.when(z != w)
        def _():
            sent(spare + 1, 1)

    @pl.when(core == 1)
    def _():
        @pl.when(regular)
        def _():
            for z2 in others(DEPTH, z):
                sent(z2 * OWN + y, 4)

        @pl.when((y == 0) & (z != w))
        def _():
            sent(spare, 4)

        for q in (1, 3):

            @pl.when(y != q)
            def _():
                for z2 in range(DEPTH):
                    sent(z2 * OWN + q, 1)

        @pl.when(y != 0)
        def _():
            sent(spare, 1)


def shards(spectra, sources):
    base, rot = tables()
    anywhere = pl.BlockSpec(memory_space=pl.ANY)
    vmem = pltpu.VMEM
    dma = pltpu.SemaphoreType.DMA
    return pl.pallas_call(
        kernel,
        out_shape=jax.ShapeDtypeStruct((NSRC // WINDOWS, CHAN, LAGS), F32),
        in_specs=[anywhere, pl.BlockSpec(memory_space=pltpu.SMEM), anywhere, anywhere],
        out_specs=pl.BlockSpec(memory_space=vmem),
        scratch_shapes=[
            vmem((1, CHAN, 2, BINS), F32),
            vmem((TILES, 8, 128), F32),
            vmem((RECV, 8, 128), F32),
            vmem((WINDOWS, OWN, 8, 128), F32),
            vmem((ITEMS, 2 * NSRC, 128), F32),
            vmem((256, WIDE), F32),
            vmem((WORK, 8, WIDE), F32),
            vmem((WORK * 256, WIDE), BF16),
            vmem((WORK * 256, WIDE), BF16),
            vmem((128, WORK * 256), BF16),
            vmem((CUTS * WINDOWS, 8, CUT), F32),
            vmem((WINDOWS, CUTS, 8, CUT), F32),
            dma((4,)),
            dma((2,)),
            dma,
            dma,
            dma,
            dma,
            dma((ITEMS,)),
            dma((ITEMS,)),
            dma,
            dma,
        ],
        compiler_params=pltpu.CompilerParams(
            collective_id=0, has_side_effects=True, vmem_limit_bytes=32 * 1024 * 1024
        ),
    )(spectra, sources, jnp.asarray(base), jnp.asarray(rot))


def solution(mesh):
    in_specs = (P("win", "recv", None, None), P())
    out_specs = P("win", "recv", None)
    return jax.shard_map(shards, mesh=mesh, in_specs=in_specs, out_specs=out_specs, check_vma=False)
```

```python
import math

import jax
import jax.numpy as jnp
import numpy as np
from jax import lax
from jax.experimental import pallas as pl
from jax.experimental.pallas import tpu as pltpu
from jax.sharding import PartitionSpec as P

BINS = 4352
NFFT = 16384
FIRST = 256
HALF = 500
LAGS = 2 * HALF + 1
NSRC = 16
WINDOWS = 8
CHAN = 4
ROWS = 4
RECV = 64
TILES = BINS // 128
ITEMS = TILES + 1
PART = NSRC // 2
WIDE = 512
CUT = 256
GROUP = 17
FIRST_PART = 17
MARKER = 21
SPARE = RECV // 2
MESH = pl.DeviceIdType.MESH
F32 = jnp.float32
BF16 = jnp.bfloat16


def tables():
    lags = np.arange(WIDE, dtype=np.int64)
    turn = 2.0 * np.pi / NFFT
    inner = (np.arange(128)[:, None] * lags[None, :]) % NFFT * turn
    base = np.concatenate([np.cos(inner), np.sin(inner)]).astype(np.float32)
    first = FIRST + 128 * np.arange(TILES, dtype=np.int64)
    outer = (first[:, None] * lags[None, :]) % NFFT * turn
    rot = np.zeros((TILES, 8, WIDE), np.float32)
    rot[:, 0] = np.cos(outer)
    rot[:, 1] = np.sin(outer)
    taper = np.sin(np.pi * (np.arange(BINS) + 0.5) / BINS) / math.sqrt(WINDOWS * BINS)
    rot[:, 2, :128] = taper.reshape(TILES, 128)
    return base, rot


def holder_of(t):
    return jnp.where(t < SPARE, 2 * t + lax.rem(t + lax.div(t, ROWS), 2), 1 + 10 * (t - SPARE))


def split(value):
    high = value.astype(BF16)
    return high, (value - high.astype(F32)).astype(BF16)


def kernel(
    spec_hbm, src_hbm, base_hbm, rot_hbm, out,
    spec, src, heard, mark, picked, items, chans, scales, base, rot, thi, tlo, mirror, cross, acc, part, parts,
    load_sem, hear_send, hear_recv, chip_send, chip_recv, item_send, item_recv, part_send, part_recv,
):
    r = lax.axis_index("recv")
    w = lax.axis_index("win")
    core = lax.rem(r, 2)
    first = r - core
    keeps = lax.div(w, WINDOWS // 2)
    regular = core == lax.rem(lax.div(r, 2) + lax.div(r, 2 * ROWS), 2)
    holder = regular | (r == 1) | (r == 11) | (r == 21)
    mine = jnp.where(regular, lax.div(r, 2), SPARE + lax.div(r, 10))
    own = core == keeps

    loads = [
        pltpu.make_async_copy(spec_hbm.at[0], spec.at[core], load_sem.at[0]),
        pltpu.make_async_copy(src_hbm, src, load_sem.at[1]),
        pltpu.make_async_copy(base_hbm, base, load_sem.at[2]),
        pltpu.make_async_copy(rot_hbm, rot, load_sem.at[3]),
    ]
    for load in loads:
        load.start()

    barrier = pltpu.get_barrier_semaphore()

    def greet(r2, w2):
        pl.semaphore_signal(barrier, inc=1, device_id=(r2, w2), device_id_type=MESH)

    greet(first + 1 - core, w)
    for d in range(1, WINDOWS):
        greet(first + keeps, lax.rem(w + d, WINDOWS))

    @pl.when(jnp.logical_not(own))
    def _():
        greet(first + keeps, w)

    @pl.when(holder)
    def _():
        def one(i, carry):
            greet(lax.rem(r + i, RECV), w)
            return carry

        lax.fori_loop(1, RECV, one, 0)

    pl.semaphore_wait(barrier, ITEMS - holder.astype(jnp.int32) + WINDOWS - own.astype(jnp.int32) + 1)

    def tell(i, carry):
        t = lax.div(i, FIRST_PART) * FIRST_PART + lax.rem(i + r, FIRST_PART)
        piece = spec_hbm.at[0, :, :, pl.ds(pl.multiple_of(t * 128, 128), 128)]

        r2 = holder_of(t)

        @pl.when(r2 == r)
        def _():
            pltpu.make_async_copy(piece, heard.at[r], hear_recv).start()

        @pl.when(r2 != r)
        def _():
            pltpu.make_async_remote_copy(
                piece, heard.at[r], hear_send, hear_recv, device_id=(r2, w), device_id_type=MESH
            ).start()

        return carry

    lax.fori_loop(0, TILES, tell, 0)
    chip = pltpu.make_async_remote_copy(
        spec_hbm.at[0], spec.at[core], chip_send, chip_recv, device_id=(first + 1 - core, w), device_id_type=MESH
    )
    chip.start()

    def shape(cc, c):
        both = spec[cc, c]
        power = jnp.sum(both * both, axis=(0, 1), keepdims=True) / BINS
        scale = jnp.broadcast_to(lax.rsqrt(power + 1e-06), (2, 128))
        for half in range(2):
            scales[cc, CHAN * half + c : CHAN * half + c + 1, :] = scale[0:1]
        for t in range(TILES):
            chans[cc, t, c : c + 1, :] = both[0:1, 128 * t : 128 * t + 128]
            chans[cc, t, CHAN + c : CHAN + c + 1, :] = both[1:2, 128 * t : 128 * t + 128]
        return scale

    loads[0].wait()
    for c in range(CHAN):
        mark[c] = shape(core, c)

    @pl.when(r == MARKER)
    def _():
        pltpu.make_async_copy(mark, heard.at[r], hear_recv).start()

    @pl.when(r != MARKER)
    def _():
        pltpu.make_async_remote_copy(
            mark, heard.at[r], hear_send, hear_recv, device_id=(MARKER, w), device_id_type=MESH
        ).start()

    loads[2].wait()
    loads[3].wait()

    def table(i, carry):
        u = lax.div(i, 8)
        row = pl.multiple_of(lax.rem(i, 8) * 16, 16)
        ct = rot[u, 0:1, :]
        st = rot[u, 1:2, :]
        cb = base[pl.ds(row, 16), :]
        sb = base[pl.ds(row + 128, 16), :]
        place = pl.ds(pl.multiple_of(u * 128 + row, 16), 16)
        thi[0, place, :], tlo[0, place, :] = split(cb * ct - sb * st)
        thi[1, place, :], tlo[1, place, :] = split(sb * ct + cb * st)
        return carry

    lax.fori_loop(0, TILES * 8, table, 0)

    loads[1].wait()

    @pl.when(holder)
    def _():
        pltpu.make_async_copy(heard, heard, hear_recv).wait()
        for k in range(NSRC):
            s = src[k]
            pair = heard[lax.shift_right_logical(s, 2), lax.bitwise_and(s, 3)]
            picked[k // PART, k % PART : k % PART + 1, :] = pair[0:1]
            picked[k // PART, PART + k % PART : PART + k % PART + 1, :] = pair[1:2]
        pltpu.make_async_copy(picked.at[core], items.at[mine], item_recv.at[mine]).start()

        def spread(i, carry):
            r2 = lax.div(i, 8) * 8 + lax.rem(r + i, 8)

            @pl.when(r2 != r)
            def _():
                pltpu.make_async_remote_copy(
                    picked.at[lax.rem(r2, 2)], items.at[mine], item_send, item_recv.at[mine], device_id=(r2, w), device_id_type=MESH
                ).start()

            return carry

        lax.fori_loop(0, RECV, spread, 0)

    chip.wait()
    for c in range(CHAN):
        shape(1 - core, c)

    def mirrored(i, carry):
        row = pl.multiple_of(i * 16, 16)
        m = lax.broadcasted_iota(jnp.int32, (16, WIDE), 0) + row
        j = lax.broadcasted_iota(jnp.int32, (16, WIDE), 1)
        mirror[pl.ds(row, 16), :] = jnp.where((m + j == HALF) & (m > 0), 1.0, 0.0).astype(BF16)
        return carry

    lax.fori_loop(0, WIDE // 16, mirrored, 0)

    upper = lax.broadcasted_iota(jnp.int32, (8, 128), 0) < CHAN

    def tile(t, carry):
        taper = rot[t, 2:3, 0:128]
        col = pl.ds(pl.multiple_of(t * 128, 128), 128)
        for cc in range(2):
            chan = chans[cc, t] * taper
            turned = pltpu.roll(chan, CHAN, 0)
            plus = jnp.where(upper, chan, -chan)
            pair = [
                items[t, k : k + 1, :] * plus + items[t, PART + k : PART + k + 1, :] * turned for k in range(PART)
            ]
            for p in range(2):
                re, im = [], []
                for g in (2 * p, 2 * p + 1):
                    a, b = pair[2 * g], pair[2 * g + 1]
                    re.append(jnp.where(upper, a, pltpu.roll(b, CHAN, 0)))
                    im.append(jnp.where(upper, pltpu.roll(a, CHAN, 0), b))
                at = 32 * cc + 16 * p
                for j, value in enumerate((re, im)):
                    high, low = split(jnp.concatenate(value, axis=0))
                    cross[j, at : at + 16, col] = high
                    cross[j, 64 + at : 64 + at + 16, col] = low
        return carry

    def arrived(t):
        pltpu.make_async_copy(items.at[t], items.at[t], item_recv.at[t]).wait()

    for start in range(0, TILES, GROUP):
        stop = min(start + GROUP, TILES)
        for t in range(start, stop):
            arrived(t)
        lax.fori_loop(start, stop, tile, 0)
        if stop == TILES:
            arrived(TILES)
        bins = slice(128 * start, 128 * stop)
        for n in range(4):
            j, cols = n // 2, slice(CUT * (n % 2), CUT * (n % 2) + CUT)
            both = jnp.dot(cross[j, :, bins], thi[j, bins, cols], preferred_element_type=F32)
            low = jnp.dot(cross[j, 0:64, bins], tlo[j, bins, cols], preferred_element_type=F32)
            value = both[0:64] + both[64:128] + low
            if start > 0:
                value = value + acc[n]
            if stop < TILES:
                acc[n] = value
                continue
            for g in range(8):
                cc, pair = g // 4, g % 4
                one = items[TILES, 2 * pair : 2 * pair + 1, :]
                two = items[TILES, 2 * pair + 1 : 2 * pair + 2, :]
                scale = jnp.where(upper, one, two) * scales[cc]
                part[n * 8 + g] = value[8 * g : 8 * g + 8] * jnp.concatenate([scale, scale], axis=1)
            for g in range(8):
                r2, w2 = first + g // 4, core * 4 + g % 4
                self = (r2 == r) & (w2 == w)

                @pl.when(self)
                def _(n=n, g=g):
                    pltpu.make_async_copy(part.at[n * 8 + g], parts.at[w, n], part_recv).start()

                @pl.when(jnp.logical_not(self))
                def _(n=n, g=g, r2=r2, w2=w2):
                    pltpu.make_async_remote_copy(
                        part.at[n * 8 + g], parts.at[w, n], part_send, part_recv, device_id=(r2, w2), device_id_type=MESH
                    ).start()

    pltpu.make_async_copy(parts, parts, part_recv).wait()
    total = []
    for n in range(4):
        value = parts[0, n]
        for v in range(1, WINDOWS):
            value = value + parts[v, n]
        total.append(value)
    even = jnp.concatenate(total[0:2], axis=1)
    odd = jnp.concatenate(total[2:4], axis=1)
    before = even + odd
    one = before.astype(BF16)
    rest = before - one.astype(F32)
    two = rest.astype(BF16)
    three = (rest - two.astype(F32)).astype(BF16)
    thrice = jnp.dot(jnp.concatenate([one, two, three], axis=0), mirror[...], preferred_element_type=F32)
    before = thrice[0:8] + thrice[8:16] + thrice[16:24]
    after = pltpu.roll(even - odd, HALF, 1)
    lane = lax.broadcasted_iota(jnp.int32, (8, WIDE), 1)
    left = jnp.where(lane < HALF, before, after)
    for k in range(2):
        out[k, :, 0:WIDE] = left[CHAN * k : CHAN * k + CHAN]
        out[k, :, WIDE:LAGS] = after[CHAN * k : CHAN * k + CHAN, 0 : LAGS - WIDE]

    @pl.when(holder)
    def _():
        pltpu.make_async_copy(heard.at[pl.ds(0, ITEMS - 1)], heard.at[pl.ds(0, ITEMS - 1)], hear_send).wait()
        pltpu.make_async_copy(items.at[pl.ds(0, RECV - 1)], items.at[pl.ds(0, RECV - 1)], item_send).wait()

    @pl.when(jnp.logical_not(holder))
    def _():
        pltpu.make_async_copy(heard.at[pl.ds(0, ITEMS)], heard.at[pl.ds(0, ITEMS)], hear_send).wait()

    @pl.when(own)
    def _():
        pltpu.make_async_copy(part.at[pl.ds(0, 28)], part.at[pl.ds(0, 28)], part_send).wait()

    @pl.when(jnp.logical_not(own))
    def _():
        pltpu.make_async_copy(part, part, part_send).wait()


def shards(spectra, sources):
    base, rot = tables()
    anywhere = pl.BlockSpec(memory_space=pl.ANY)
    vmem = pltpu.VMEM
    dma = pltpu.SemaphoreType.DMA
    return pl.pallas_call(
        kernel,
        out_shape=jax.ShapeDtypeStruct((NSRC // WINDOWS, CHAN, LAGS), F32),
        in_specs=[anywhere] * 4,
        out_specs=pl.BlockSpec(memory_space=vmem),
        scratch_shapes=[
            vmem((2, CHAN, 2, BINS), F32),
            pltpu.SMEM((NSRC,), jnp.int32),
            vmem((RECV, CHAN, 2, 128), F32),
            vmem((CHAN, 2, 128), F32),
            vmem((2, 2 * PART, 128), F32),
            vmem((RECV, 2 * PART, 128), F32),
            vmem((2, TILES, 8, 128), F32),
            vmem((2, 8, 128), F32),
            vmem((256, WIDE), F32),
            vmem((TILES, 8, WIDE), F32),
            vmem((2, BINS, WIDE), BF16),
            vmem((2, BINS, WIDE), BF16),
            vmem((WIDE, WIDE), BF16),
            vmem((2, 128, BINS), BF16),
            vmem((4, 64, CUT), F32),
            vmem((32, 8, CUT), F32),
            vmem((WINDOWS, 4, 8, CUT), F32),
            dma((4,)),
            dma,
            dma,
            dma,
            dma,
            dma,
            dma((ITEMS,)),
            dma,
            dma,
        ],
        compiler_params=pltpu.CompilerParams(
            collective_id=0, has_side_effects=True, vmem_limit_bytes=60 * 1024 * 1024
        ),
    )(spectra, sources, jnp.asarray(base), jnp.asarray(rot))


def solution(mesh):
    in_specs = (P("win", "recv", None, None), P())
    out_specs = P("win", "recv", None)
    return jax.shard_map(shards, mesh=mesh, in_specs=in_specs, out_specs=out_specs, check_vma=False)
```

```python
import math

import jax
import jax.numpy as jnp
import numpy as np
from jax import lax
from jax.experimental import pallas as pl
from jax.experimental.pallas import tpu as pltpu
from jax.sharding import PartitionSpec as P

BINS = 4352
NFFT = 16384
FIRST = 256
HALF = 500
LAGS = 2 * HALF + 1
NSRC = 16
WINDOWS = 8
CHAN = 4
ROWS = 4
RECV = 64
TILES = BINS // 128
ITEMS = TILES + 1
PART = NSRC // 2
WIDE = 512
CUT = 256
GROUPS = ((0, 12), (12, 20), (20, 28), (28, 34))
FIRST_PART = 17
MARKER = 34
URGENT_Z = (0, 1, 2, 3, 3.5, 4.5, 5.5, 6)
URGENT_Y = (-0.9, -0.3, 0.4, 0)
ORDER = sorted(range(RECV), key=lambda r2: URGENT_Z[r2 // 8] + URGENT_Y[r2 // 2 % 4])
SPARE = RECV // 2
MESH = pl.DeviceIdType.MESH
F32 = jnp.float32
BF16 = jnp.bfloat16


def tables():
    lags = np.arange(WIDE, dtype=np.int64)
    turn = 2.0 * np.pi / NFFT
    inner = (np.arange(128)[:, None] * lags[None, :]) % NFFT * turn
    base = np.concatenate([np.cos(inner), np.sin(inner)]).astype(np.float32)
    first = FIRST + 128 * np.arange(TILES, dtype=np.int64)
    outer = (first[:, None] * lags[None, :]) % NFFT * turn
    rot = np.zeros((TILES, 8, WIDE), np.float32)
    rot[:, 0] = np.cos(outer)
    rot[:, 1] = np.sin(outer)
    taper = np.sin(np.pi * (np.arange(BINS) + 0.5) / BINS) / math.sqrt(WINDOWS * BINS)
    rot[:, 2, :128] = taper.reshape(TILES, 128)
    return base, rot


def holder_of(t):
    return t


def split(value):
    high = value.astype(BF16)
    return high, (value - high.astype(F32)).astype(BF16)


def kernel(
    spec_hbm, src_hbm, base_hbm, rot_hbm, out,
    spec, src, heard, mark, picked, items, chans, scales, base, rot, thi, tlo, mirror, cross, acc, part, parts,
    load_sem, hear_send, hear_recv, chip_send, chip_recv, item_send, item_recv, part_send, part_recv,
):
    r = lax.axis_index("recv")
    w = lax.axis_index("win")
    core = lax.rem(r, 2)
    first = r - core
    keeps = lax.div(w, WINDOWS // 2)
    holder = r < ITEMS
    mine = r
    own = core == keeps

    loads = [
        pltpu.make_async_copy(spec_hbm.at[0], spec.at[core], load_sem.at[0]),
        pltpu.make_async_copy(src_hbm, src, load_sem.at[1]),
        pltpu.make_async_copy(base_hbm, base, load_sem.at[2]),
        pltpu.make_async_copy(rot_hbm, rot, load_sem.at[3]),
    ]
    for load in loads:
        load.start()

    barrier = pltpu.get_barrier_semaphore()

    def greet(r2, w2):
        pl.semaphore_signal(barrier, inc=1, device_id=(r2, w2), device_id_type=MESH)

    @pl.when(holder)
    def _():
        def one(i, carry):
            step = i + RECV // 2
            greet(lax.bitwise_and(r + jnp.where(step < RECV, step, step - RECV + 1), RECV - 1), w)
            return carry

        lax.fori_loop(0, RECV - 1, one, 0)

    greet(first + 1 - core, w)
    for d in range(1, WINDOWS):
        greet(first + keeps, lax.bitwise_and(w + d, WINDOWS - 1))

    @pl.when(jnp.logical_not(own))
    def _():
        greet(first + keeps, w)

    def shape(cc, c):
        both = spec[cc, c]
        power = jnp.sum(both * both, axis=(0, 1), keepdims=True) / BINS
        scale = jnp.broadcast_to(lax.rsqrt(power + 1e-06), (2, 128))
        for half in range(2):
            scales[cc, CHAN * half + c : CHAN * half + c + 1, :] = scale[0:1]
        for t in range(TILES):
            chans[cc, t, c : c + 1, :] = both[0:1, 128 * t : 128 * t + 128]
            chans[cc, t, CHAN + c : CHAN + c + 1, :] = both[1:2, 128 * t : 128 * t + 128]
        return scale

    loads[0].wait()
    for c in range(CHAN):
        mark[c] = shape(core, c)

    pl.semaphore_wait(barrier, ITEMS - holder.astype(jnp.int32) + WINDOWS - own.astype(jnp.int32) + 1)

    def tell(i, carry):
        t = turn + lax.rem(i, FIRST_PART)
        t = jnp.where(t < FIRST_PART, t, t - FIRST_PART) + lax.div(i, FIRST_PART) * FIRST_PART
        piece = spec.at[core, :, :, pl.ds(pl.multiple_of(t * 128, 128), 128)]

        r2 = holder_of(t)

        @pl.when(r2 == r)
        def _():
            pltpu.make_async_copy(piece, heard.at[r], hear_recv).start()

        @pl.when(r2 != r)
        def _():
            pltpu.make_async_remote_copy(
                piece, heard.at[r], hear_send, hear_recv, device_id=(r2, w), device_id_type=MESH
            ).start()

        return carry

    turn = lax.rem(r, FIRST_PART)
    for i in range(TILES):
        tell(i, 0)
    chip = pltpu.make_async_remote_copy(
        spec_hbm.at[0], spec.at[core], chip_send, chip_recv, device_id=(first + 1 - core, w), device_id_type=MESH
    )
    chip.start()

    @pl.when(r == MARKER)
    def _():
        pltpu.make_async_copy(mark, heard.at[r], hear_recv).start()

    @pl.when(r != MARKER)
    def _():
        pltpu.make_async_remote_copy(
            mark, heard.at[r], hear_send, hear_recv, device_id=(MARKER, w), device_id_type=MESH
        ).start()

    loads[2].wait()
    loads[3].wait()

    z = lax.shift_right_logical(r, 3)

    def tile_at(p):
        near = p
        return jnp.where(p < SPARE, near, p)

    def table(i, carry):
        p = lax.shift_right_logical(i, 3)
        u = tile_at(p)
        row = pl.multiple_of(lax.bitwise_and(i, 7) * 16, 16)
        ct = rot[u, 0:1, :]
        st = rot[u, 1:2, :]
        cb = base[pl.ds(row, 16), :]
        sb = base[pl.ds(row + 128, 16), :]
        place = pl.ds(pl.multiple_of(p * 128 + row, 16), 16)
        thi[0, place, :], tlo[0, place, :] = split(cb * ct - sb * st)
        thi[1, place, :], tlo[1, place, :] = split(sb * ct + cb * st)
        return carry

    lax.fori_loop(0, TILES * 8, table, 0)

    loads[1].wait()

    @pl.when(holder)
    def _():
        pltpu.make_async_copy(heard, heard, hear_recv).wait()
        for k in range(NSRC):
            s = src[k]
            pair = heard[lax.shift_right_logical(s, 2), lax.bitwise_and(s, 3)]
            picked[k // PART, k % PART : k % PART + 1, :] = pair[0:1]
            picked[k // PART, PART + k % PART : PART + k % PART + 1, :] = pair[1:2]
        pltpu.make_async_copy(picked.at[core], items.at[mine], item_recv.at[mine]).start()

        def spread(i, carry):
            r2 = i

            @pl.when(r2 != r)
            def _():
                pltpu.make_async_remote_copy(
                    picked.at[i % 2], items.at[mine], item_send, item_recv.at[mine], device_id=(r2, w), device_id_type=MESH
                ).start()

            return carry

        for i in ORDER:
            spread(i, 0)

    chip.wait()
    for c in range(CHAN):
        shape(1 - core, c)

    def mirrored(i, carry):
        row = pl.multiple_of(i * 16, 16)
        m = lax.broadcasted_iota(jnp.int32, (16, WIDE), 0) + row
        j = lax.broadcasted_iota(jnp.int32, (16, WIDE), 1)
        mirror[pl.ds(row, 16), :] = jnp.where((m + j == HALF) & (m > 0), 1.0, 0.0).astype(BF16)
        return carry

    lax.fori_loop(0, WIDE // 16, mirrored, 0)

    x = lax.shift_right_logical(w, 1)
    ahead = jnp.where((lax.bitwise_and(2 * core + 1 - x + 4, 3) == 2) | (2 * core == x), 2, 0)
    upper = lax.broadcasted_iota(jnp.int32, (8, 128), 0) < CHAN

    def tile(p, carry):
        t = tile_at(p)
        taper = rot[t, 2:3, 0:128]
        col = pl.ds(pl.multiple_of(p * 128, 128), 128)
        for cc in range(2):
            chan = chans[cc, t] * taper
            turned = pltpu.roll(chan, CHAN, 0)
            plus = jnp.where(upper, chan, -chan)
            pair = [
                items[t, k : k + 1, :] * plus + items[t, PART + k : PART + k + 1, :] * turned for k in range(PART)
            ]
            for h in range(2):
                re, im = [], []
                for g in (2 * h, 2 * h + 1):
                    a, b = pair[2 * g], pair[2 * g + 1]
                    re.append(jnp.where(upper, a, pltpu.roll(b, CHAN, 0)))
                    im.append(jnp.where(upper, pltpu.roll(a, CHAN, 0), b))
                at = 32 * cc + 16 * h
                for j, value in enumerate((re, im)):
                    high, low = split(jnp.concatenate(value, axis=0))
                    cross[j, at : at + 16, col] = high
                    cross[j, 64 + at : 64 + at + 16, col] = low
        return carry

    def arrived(t):
        pltpu.make_async_copy(items.at[t], items.at[t], item_recv.at[t]).wait()

    for start, stop in GROUPS:
        for p in range(start, stop):
            arrived(tile_at(p))
        lax.fori_loop(start, stop, tile, 0)
        if stop == TILES:
            arrived(TILES)
        bins = slice(128 * start, 128 * stop)
        for n in range(4):
            j, cols = n // 2, slice(CUT * (n % 2), CUT * (n % 2) + CUT)
            both = jnp.dot(cross[j, :, bins], thi[j, bins, cols], preferred_element_type=F32)
            low = jnp.dot(cross[j, 0:64, bins], tlo[j, bins, cols], preferred_element_type=F32)
            value = both[0:64] + both[64:128] + low
            if start > 0:
                value = value + acc[n]
            if stop < TILES:
                acc[n] = value
                continue
            for g in range(8):
                cc, pair = g // 4, g % 4
                one = items[TILES, 2 * pair : 2 * pair + 1, :]
                two = items[TILES, 2 * pair + 1 : 2 * pair + 2, :]
                scale = jnp.where(upper, one, two) * scales[cc]
                part[n * 8 + g] = value[8 * g : 8 * g + 8] * jnp.concatenate([scale, scale], axis=1)
            for g in range(8):
                pair = lax.bitwise_xor(g // 2, ahead)
                r2, w2 = first + g % 2, core * 4 + pair
                g = n * 8 + (g % 2) * 4 + pair
                self = (r2 == r) & (w2 == w)

                @pl.when(self)
                def _(n=n, g=g):
                    pltpu.make_async_copy(part.at[g], parts.at[n, w], part_recv.at[n]).start()

                @pl.when(jnp.logical_not(self))
                def _(n=n, g=g, r2=r2, w2=w2):
                    pltpu.make_async_remote_copy(
                        part.at[g], parts.at[n, w], part_send, part_recv.at[n], device_id=(r2, w2), device_id_type=MESH
                    ).start()

    total = []
    for n in range(4):
        pltpu.make_async_copy(parts.at[n], parts.at[n], part_recv.at[n]).wait()
        value = parts[n, 0]
        for v in range(1, WINDOWS):
            value = value + parts[n, v]
        total.append(value)
    even = jnp.concatenate(total[0:2], axis=1)
    odd = jnp.concatenate(total[2:4], axis=1)
    before = even + odd
    one = before.astype(BF16)
    rest = before - one.astype(F32)
    two = rest.astype(BF16)
    three = (rest - two.astype(F32)).astype(BF16)
    thrice = jnp.dot(jnp.concatenate([one, two, three], axis=0), mirror[...], preferred_element_type=F32)
    before = thrice[0:8] + thrice[8:16] + thrice[16:24]
    after = pltpu.roll(even - odd, HALF, 1)
    lane = lax.broadcasted_iota(jnp.int32, (8, WIDE), 1)
    left = jnp.where(lane < HALF, before, after)
    for k in range(2):
        out[k, :, 0:WIDE] = left[CHAN * k : CHAN * k + CHAN]
        out[k, :, WIDE:LAGS] = after[CHAN * k : CHAN * k + CHAN, 0 : LAGS - WIDE]

    @pl.when(holder)
    def _():
        pltpu.make_async_copy(heard.at[pl.ds(0, ITEMS - 1)], heard.at[pl.ds(0, ITEMS - 1)], hear_send).wait()
        pltpu.make_async_copy(items.at[pl.ds(0, RECV - 1)], items.at[pl.ds(0, RECV - 1)], item_send).wait()

    @pl.when(jnp.logical_not(holder))
    def _():
        pltpu.make_async_copy(heard.at[pl.ds(0, ITEMS)], heard.at[pl.ds(0, ITEMS)], hear_send).wait()

    @pl.when(own)
    def _():
        pltpu.make_async_copy(part.at[pl.ds(0, 28)], part.at[pl.ds(0, 28)], part_send).wait()

    @pl.when(jnp.logical_not(own))
    def _():
        pltpu.make_async_copy(part, part, part_send).wait()


def shards(spectra, sources):
    base, rot = tables()
    anywhere = pl.BlockSpec(memory_space=pl.ANY)
    vmem = pltpu.VMEM
    dma = pltpu.SemaphoreType.DMA
    return pl.pallas_call(
        kernel,
        out_shape=pltpu.VMEM((NSRC // WINDOWS, CHAN, LAGS), F32),
        in_specs=[anywhere] * 4,
        out_specs=pl.BlockSpec(memory_space=vmem),
        scratch_shapes=[
            vmem((2, CHAN, 2, BINS), F32),
            pltpu.SMEM((NSRC,), jnp.int32),
            vmem((RECV, CHAN, 2, 128), F32),
            vmem((CHAN, 2, 128), F32),
            vmem((2, 2 * PART, 128), F32),
            vmem((RECV, 2 * PART, 128), F32),
            vmem((2, TILES, 8, 128), F32),
            vmem((2, 8, 128), F32),
            vmem((256, WIDE), F32),
            vmem((TILES, 8, WIDE), F32),
            vmem((2, BINS, WIDE), BF16),
            vmem((2, BINS, WIDE), BF16),
            vmem((WIDE, WIDE), BF16),
            vmem((2, 128, BINS), BF16),
            vmem((4, 64, CUT), F32),
            vmem((32, 8, CUT), F32),
            vmem((4, WINDOWS, 8, CUT), F32),
            dma((4,)),
            dma,
            dma,
            dma,
            dma,
            dma,
            dma((ITEMS,)),
            dma,
            dma((4,)),
        ],
        compiler_params=pltpu.CompilerParams(
            collective_id=0, has_side_effects=True, vmem_limit_bytes=60 * 1024 * 1024
        ),
    )(spectra, sources, jnp.asarray(base), jnp.asarray(rot))


def solution(mesh):
    in_specs = (P("win", "recv", None, None), P())
    out_specs = P("win", "recv", None)
    return jax.shard_map(shards, mesh=mesh, in_specs=in_specs, out_specs=out_specs, check_vma=False)
```

```python
import math

import jax
import jax.numpy as jnp
import numpy as np
from jax import lax
from jax.experimental import pallas as pl
from jax.experimental.pallas import tpu as pltpu
from jax.sharding import PartitionSpec as P

BINS = 4352
NFFT = 16384
FIRST = 256
HALF = 500
LAGS = 2 * HALF + 1
NSRC = 16
WINDOWS = 8
CHAN = 4
ROWS = 4
RECV = 64
TILES = BINS // 128
ITEMS = TILES + 1
TEAM = 4
PART = NSRC // TEAM
WIDE = 512
CUT = 256
GROUPS = ((0, 12), (12, 20), (20, 28), (28, 34))
FIRST_PART = 17
MARKER = 34
URGENT_Z = (0, 0.3, 2, 2.3, 4, 4.3, 5, 5.3)
URGENT_Y = (-0.2, -0.1, 0.1, 0)
ORDER = sorted(range(RECV), key=lambda r2: URGENT_Z[r2 // 8] + URGENT_Y[r2 // 2 % 4])
SPARE = RECV // 2
MESH = pl.DeviceIdType.MESH
F32 = jnp.float32
BF16 = jnp.bfloat16


def tables():
    lags = np.arange(WIDE, dtype=np.int64)
    turn = 2.0 * np.pi / NFFT
    inner = (np.arange(128)[:, None] * lags[None, :]) % NFFT * turn
    base = np.concatenate([np.cos(inner), np.sin(inner)]).astype(np.float32)
    first = FIRST + 128 * np.arange(TILES, dtype=np.int64)
    outer = (first[:, None] * lags[None, :]) % NFFT * turn
    rot = np.zeros((TILES, 8, WIDE), np.float32)
    rot[:, 0] = np.cos(outer)
    rot[:, 1] = np.sin(outer)
    taper = np.sin(np.pi * (np.arange(BINS) + 0.5) / BINS) / math.sqrt(WINDOWS * BINS)
    rot[:, 2, :128] = taper.reshape(TILES, 128)
    return base, rot


def member_of(r):
    return (r & 1) * 2 + ((r >> 3) & 1)


def split(value):
    high = value.astype(BF16)
    return high, (value - high.astype(F32)).astype(BF16)


def kernel(
    spec_hbm, src_hbm, base_hbm, rot_hbm, out,
    spec, src, heard, mark, picked, items, chans, scales, base, rot, thi, tlo, mirror, cross, acc, part, parts,
    load_sem, hear_send, hear_recv, share_send, share_recv, item_send, item_recv, part_send, part_recv,
):
    r = lax.axis_index("recv")
    w = lax.axis_index("win")
    core = lax.rem(r, 2)
    me = member_of(r)
    team = r - core - 8 * (me & 1)

    def member(q):
        return team + 8 * (q & 1) + (q >> 1)

    keeps = jnp.where(w < TEAM, w, WINDOWS - 1 - w)
    holder = r < ITEMS
    own = me == keeps
    other_core = r + 1 - 2 * core
    other_chip = member(me ^ 1)

    loads = [
        pltpu.make_async_copy(spec_hbm.at[0], spec.at[me], load_sem.at[0]),
        pltpu.make_async_copy(src_hbm, src, load_sem.at[1]),
        pltpu.make_async_copy(base_hbm, base, load_sem.at[2]),
        pltpu.make_async_copy(rot_hbm, rot, load_sem.at[3]),
    ]
    for load in loads:
        load.start()

    barrier = pltpu.get_barrier_semaphore()

    def greet(r2, w2):
        pl.semaphore_signal(barrier, inc=1, device_id=(r2, w2), device_id_type=MESH)

    @pl.when(holder)
    def _():
        def one(i, carry):
            step = i + RECV // 2
            greet(lax.bitwise_and(r + jnp.where(step < RECV, step, step - RECV + 1), RECV - 1), w)
            return carry

        lax.fori_loop(0, RECV - 1, one, 0)

    greet(other_core, w)
    greet(other_chip, w)
    for d in range(1, WINDOWS):
        greet(member(keeps), lax.bitwise_and(w + d, WINDOWS - 1))

    @pl.when(jnp.logical_not(own))
    def _():
        greet(member(keeps), w)

    def shape(cc, c):
        both = spec[cc, c]
        power = jnp.sum(both * both, axis=(0, 1), keepdims=True) / BINS
        scale = jnp.broadcast_to(lax.rsqrt(power + 1e-06), (2, 128))
        for half in range(2):
            scales[cc, CHAN * half + c : CHAN * half + c + 1, :] = scale[0:1]
        for t in range(TILES):
            chans[cc, t, c : c + 1, :] = both[0:1, 128 * t : 128 * t + 128]
            chans[cc, t, CHAN + c : CHAN + c + 1, :] = both[1:2, 128 * t : 128 * t + 128]
        return scale

    loads[0].wait()
    for c in range(CHAN):
        mark[c] = shape(me, c)

    pl.semaphore_wait(barrier, ITEMS - holder.astype(jnp.int32) + WINDOWS - own.astype(jnp.int32) + 2)

    def tell(i, carry):
        t = turn + lax.rem(i, FIRST_PART)
        t = jnp.where(t < FIRST_PART, t, t - FIRST_PART) + lax.div(i, FIRST_PART) * FIRST_PART
        piece = spec.at[me, :, :, pl.ds(pl.multiple_of(t * 128, 128), 128)]

        @pl.when(t == r)
        def _():
            pltpu.make_async_copy(piece, heard.at[r], hear_recv).start()

        @pl.when(t != r)
        def _():
            pltpu.make_async_remote_copy(
                piece, heard.at[r], hear_send, hear_recv, device_id=(t, w), device_id_type=MESH
            ).start()

        return carry

    turn = lax.rem(r, FIRST_PART)
    for i in range(TILES):
        tell(i, 0)

    def share(q, r2, sem):
        return pltpu.make_async_remote_copy(
            spec.at[q], spec.at[q], share_send.at[sem], share_recv.at[sem], device_id=(r2, w), device_id_type=MESH
        )

    to_chip = share(me, other_chip, 0)
    to_core = share(me, other_core, 1)
    to_core_too = share(me ^ 1, other_core, 2)
    to_chip.start()
    to_core.start()

    @pl.when(r == MARKER)
    def _():
        pltpu.make_async_copy(mark, heard.at[r], hear_recv).start()

    @pl.when(r != MARKER)
    def _():
        pltpu.make_async_remote_copy(
            mark, heard.at[r], hear_send, hear_recv, device_id=(MARKER, w), device_id_type=MESH
        ).start()

    loads[2].wait()
    loads[3].wait()

    z = lax.shift_right_logical(r, 3)
    flip = jnp.where((z >= 2) & (z <= 5), 24, 0)

    def tile_at(p):
        return jnp.where(p < SPARE, p ^ flip, p)

    def table(i, carry):
        p = lax.shift_right_logical(i, 3)
        u = tile_at(p)
        row = pl.multiple_of(lax.bitwise_and(i, 7) * 16, 16)
        ct = rot[u, 0:1, :]
        st = rot[u, 1:2, :]
        cb = base[pl.ds(row, 16), :]
        sb = base[pl.ds(row + 128, 16), :]
        place = pl.ds(pl.multiple_of(p * 128 + row, 16), 16)
        thi[0, place, :], tlo[0, place, :] = split(cb * ct - sb * st)
        thi[1, place, :], tlo[1, place, :] = split(sb * ct + cb * st)
        return carry

    lax.fori_loop(0, TILES * 8, table, 0)

    loads[1].wait()

    @pl.when(holder)
    def _():
        pltpu.make_async_copy(heard, heard, hear_recv).wait()
        for k in range(NSRC):
            s = src[k]
            pair = heard[lax.shift_right_logical(s, 2), lax.bitwise_and(s, 3)]
            v = k // 2
            q, place = min(v, WINDOWS - 1 - v), 2 * (v // TEAM) + k % 2
            picked[q, place : place + 1, :] = pair[0:1]
            picked[q, PART + place : PART + place + 1, :] = pair[1:2]
        pltpu.make_async_copy(picked.at[me], items.at[r], item_recv.at[r]).start()

        def spread(i, carry):
            r2 = i

            @pl.when(r2 != r)
            def _():
                pltpu.make_async_remote_copy(
                    picked.at[member_of(i)], items.at[r], item_send, item_recv.at[r], device_id=(r2, w), device_id_type=MESH
                ).start()

            return carry

        for i in ORDER:
            spread(i, 0)

    to_chip.wait()
    to_core_too.start()
    for c in range(CHAN):
        shape(me ^ 1, c)
    to_core.wait()
    for c in range(CHAN):
        shape(me ^ 2, c)
    to_core_too.wait()
    for c in range(CHAN):
        shape(me ^ 3, c)

    def mirrored(i, carry):
        row = pl.multiple_of(i * 16, 16)
        m = lax.broadcasted_iota(jnp.int32, (16, WIDE), 0) + row
        j = lax.broadcasted_iota(jnp.int32, (16, WIDE), 1)
        mirror[pl.ds(row, 16), :] = jnp.where((m + j == HALF) & (m > 0), 1.0, 0.0).astype(BF16)
        return carry

    lax.fori_loop(0, WIDE // 16, mirrored, 0)

    x = w >> 1
    near_x = ((me >> 1) - x) & 3
    far_x = (3 - (me >> 1) - x) & 3
    ahead = ((far_x == 2) | (near_x == 0)).astype(jnp.int32)
    upper = lax.broadcasted_iota(jnp.int32, (8, 128), 0) < CHAN

    def tile(p, carry):
        t = tile_at(p)
        taper = rot[t, 2:3, 0:128]
        col = pl.ds(pl.multiple_of(p * 128, 128), 128)
        for cc in range(TEAM):
            chan = chans[cc, t] * taper
            turned = pltpu.roll(chan, CHAN, 0)
            plus = jnp.where(upper, chan, -chan)
            pair = [
                items[t, k : k + 1, :] * plus + items[t, PART + k : PART + k + 1, :] * turned for k in range(PART)
            ]
            re, im = [], []
            for a, b in (pair[0:2], pair[2:4]):
                re.append(jnp.where(upper, a, pltpu.roll(b, CHAN, 0)))
                im.append(jnp.where(upper, pltpu.roll(a, CHAN, 0), b))
            at = 16 * cc
            for j, value in enumerate((re, im)):
                high, low = split(jnp.concatenate(value, axis=0))
                cross[j, at : at + 16, col] = high
                cross[j, 64 + at : 64 + at + 16, col] = low
        return carry

    def arrived(t):
        pltpu.make_async_copy(items.at[t], items.at[t], item_recv.at[t]).wait()

    for start, stop in GROUPS:
        for p in range(start, stop):
            arrived(tile_at(p))
        lax.fori_loop(start, stop, tile, 0)
        if stop == TILES:
            arrived(TILES)
        bins = slice(128 * start, 128 * stop)
        for n in range(4):
            j, cols = n % 2, slice(CUT * (n // 2), CUT * (n // 2) + CUT)
            both = jnp.dot(cross[j, :, bins], thi[j, bins, cols], preferred_element_type=F32)
            low = jnp.dot(cross[j, 0:64, bins], tlo[j, bins, cols], preferred_element_type=F32)
            value = both[0:64] + both[64:128] + low
            if start > 0:
                value = value + acc[n]
            if stop < TILES:
                acc[n] = value
                continue
            for g in range(8):
                cc, j = g // 2, g % 2
                scale = jnp.where(upper, items[TILES, 2 * j : 2 * j + 1, :], items[TILES, 2 * j + 1 : 2 * j + 2, :])
                scale = scale * scales[cc]
                part[n * 8 + g] = value[8 * g : 8 * g + 8] * jnp.concatenate([scale, scale], axis=1)
            for i in range(8):
                cc, j = me ^ (1, 3, 2, 0)[i % 4], ahead ^ (i // 4)
                r2, w2 = member(cc), jnp.where(j == 0, me, WINDOWS - 1 - me)
                g = n * 8 + cc * 2 + j
                self = (r2 == r) & (w2 == w)

                @pl.when(self)
                def _(n=n, g=g):
                    pltpu.make_async_copy(part.at[g], parts.at[n, w], part_recv.at[n]).start()

                @pl.when(jnp.logical_not(self))
                def _(n=n, g=g, r2=r2, w2=w2):
                    pltpu.make_async_remote_copy(
                        part.at[g], parts.at[n, w], part_send, part_recv.at[n], device_id=(r2, w2), device_id_type=MESH
                    ).start()

    total = []
    for n in range(4):
        pltpu.make_async_copy(parts.at[n], parts.at[n], part_recv.at[n]).wait()
        value = parts[n, 0]
        for v in range(1, WINDOWS):
            value = value + parts[n, v]
        total.append(value)
    even = jnp.concatenate(total[0::2], axis=1)
    odd = jnp.concatenate(total[1::2], axis=1)
    before = even + odd
    one = before.astype(BF16)
    rest = before - one.astype(F32)
    two = rest.astype(BF16)
    three = (rest - two.astype(F32)).astype(BF16)
    thrice = jnp.dot(jnp.concatenate([one, two, three], axis=0), mirror[...], preferred_element_type=F32)
    before = thrice[0:8] + thrice[8:16] + thrice[16:24]
    after = pltpu.roll(even - odd, HALF, 1)
    lane = lax.broadcasted_iota(jnp.int32, (8, WIDE), 1)
    left = jnp.where(lane < HALF, before, after)
    for k in range(2):
        out[k, :, 0:WIDE] = left[CHAN * k : CHAN * k + CHAN]
        out[k, :, WIDE:LAGS] = after[CHAN * k : CHAN * k + CHAN, 0 : LAGS - WIDE]

    @pl.when(holder)
    def _():
        pltpu.make_async_copy(heard.at[pl.ds(0, ITEMS - 1)], heard.at[pl.ds(0, ITEMS - 1)], hear_send).wait()
        pltpu.make_async_copy(items.at[pl.ds(0, RECV - 1)], items.at[pl.ds(0, RECV - 1)], item_send).wait()

    @pl.when(jnp.logical_not(holder))
    def _():
        pltpu.make_async_copy(heard.at[pl.ds(0, ITEMS)], heard.at[pl.ds(0, ITEMS)], hear_send).wait()

    @pl.when(own)
    def _():
        pltpu.make_async_copy(part.at[pl.ds(0, 28)], part.at[pl.ds(0, 28)], part_send).wait()

    @pl.when(jnp.logical_not(own))
    def _():
        pltpu.make_async_copy(part, part, part_send).wait()


def shards(spectra, sources):
    base, rot = tables()
    anywhere = pl.BlockSpec(memory_space=pl.ANY)
    vmem = pltpu.VMEM
    dma = pltpu.SemaphoreType.DMA
    return pl.pallas_call(
        kernel,
        out_shape=pltpu.VMEM((NSRC // WINDOWS, CHAN, LAGS), F32),
        in_specs=[anywhere] * 4,
        out_specs=pl.BlockSpec(memory_space=vmem),
        scratch_shapes=[
            vmem((TEAM, CHAN, 2, BINS), F32),
            pltpu.SMEM((NSRC,), jnp.int32),
            vmem((RECV, CHAN, 2, 128), F32),
            vmem((CHAN, 2, 128), F32),
            vmem((TEAM, 2 * PART, 128), F32),
            vmem((RECV, 2 * PART, 128), F32),
            vmem((TEAM, TILES, 8, 128), F32),
            vmem((TEAM, 8, 128), F32),
            vmem((256, WIDE), F32),
            vmem((TILES, 8, WIDE), F32),
            vmem((2, BINS, WIDE), BF16),
            vmem((2, BINS, WIDE), BF16),
            vmem((WIDE, WIDE), BF16),
            vmem((2, 128, BINS), BF16),
            vmem((4, 64, CUT), F32),
            vmem((32, 8, CUT), F32),
            vmem((4, WINDOWS, 8, CUT), F32),
            dma((4,)),
            dma,
            dma,
            dma((3,)),
            dma((3,)),
            dma,
            dma((ITEMS,)),
            dma,
            dma((4,)),
        ],
        compiler_params=pltpu.CompilerParams(
            collective_id=0, has_side_effects=True, vmem_limit_bytes=60 * 1024 * 1024
        ),
    )(spectra, sources, jnp.asarray(base), jnp.asarray(rot))


def solution(mesh):
    in_specs = (P("win", "recv", None, None), P())
    out_specs = P("win", "recv", None)
    return jax.shard_map(shards, mesh=mesh, in_specs=in_specs, out_specs=out_specs, check_vma=False)
```

```python
import math

import jax
import jax.numpy as jnp
import numpy as np
from jax import lax
from jax.experimental import pallas as pl
from jax.experimental.pallas import tpu as pltpu
from jax.sharding import PartitionSpec as P

BINS = 4352
NFFT = 16384
FIRST = 256
HALF = 500
LAGS = 2 * HALF + 1
NSRC = 16
WINDOWS = 8
CHAN = 4
ROWS = 4
RECV = 64
TILES = BINS // 128
ITEMS = TILES + 1
TEAM = 4
PART = NSRC // TEAM
WIDE = 512
CUT = 256
GROUPS = ((0, 12), (12, 20), (20, 28), (28, 34))
NEAR = sorted(((z, y) for z in range(4) for y in range(4)), key=lambda at: at[0] + 2 * min(at[1], 4 - at[1]))
NEAR_Z = [sum(NEAR[8 * h + i][0] << (2 * i) for i in range(8)) for h in range(2)]
NEAR_Y = [sum(NEAR[8 * h + i][1] << (2 * i) for i in range(8)) for h in range(2)]
FAR = sorted(
    ((z, y, c) for z in range(8) for y in range(ROWS) for c in range(2) if z or y or c),
    key=lambda at: -min(at[0], 8 - at[0]) - 2 * min(at[1], 4 - at[1]),
)
MARKER = 32
LATE = 56
URGENT_Z = (0, 0.3, 2, 2.3, 4, 4.3, 5, 5.3)
URGENT_Y = (-0.2, -0.1, 0.1, 0)
ORDER = sorted(range(RECV), key=lambda r2: URGENT_Z[r2 // 8] + URGENT_Y[r2 // 2 % 4])
SPARE = RECV // 2
MESH = pl.DeviceIdType.MESH
F32 = jnp.float32
BF16 = jnp.bfloat16


def tables():
    lags = np.arange(WIDE, dtype=np.int64)
    turn = 2.0 * np.pi / NFFT
    inner = (np.arange(128)[:, None] * lags[None, :]) % NFFT * turn
    base = np.concatenate([np.cos(inner), np.sin(inner)]).astype(np.float32)
    first = FIRST + 128 * np.arange(TILES, dtype=np.int64)
    outer = (first[:, None] * lags[None, :]) % NFFT * turn
    rot = np.zeros((TILES, 8, WIDE), np.float32)
    rot[:, 0] = np.cos(outer)
    rot[:, 1] = np.sin(outer)
    taper = np.sin(np.pi * (np.arange(BINS) + 0.5) / BINS) / math.sqrt(WINDOWS * BINS)
    rot[:, 2, :128] = taper.reshape(TILES, 128)
    return base, rot


def member_of(r):
    return (r & 1) * 2 + ((r >> 3) & 1)


def split(value):
    high = value.astype(BF16)
    return high, (value - high.astype(F32)).astype(BF16)


def kernel(
    spec_hbm, src_hbm, base_hbm, rot_hbm, out,
    spec, src, heard, mark, picked, items, chans, base, rot, thi, tlo, mirror, cross, acc, part, parts,
    load_sem, hear_send, hear_recv, share_send, share_recv, item_send, item_recv, part_send, part_recv,
):
    r = lax.axis_index("recv")
    w = lax.axis_index("win")
    core = lax.rem(r, 2)
    me = member_of(r)
    team = r - core - 8 * (me & 1)

    def member(q):
        return team + 8 * (q & 1) + (q >> 1)

    keeps = jnp.where(w < TEAM, w, WINDOWS - 1 - w)
    holder = (r < SPARE) | (r == MARKER) | (r == LATE) | (r == LATE + 1)
    mine = jnp.where(r < SPARE, r, jnp.where(r == MARKER, TILES, SPARE + r - LATE))
    own = me == keeps
    other_core = r + 1 - 2 * core
    other_chip = member(me ^ 1)

    loads = [
        pltpu.make_async_copy(spec_hbm.at[0], spec, load_sem.at[0]),
        pltpu.make_async_copy(src_hbm, src, load_sem.at[1]),
        pltpu.make_async_copy(base_hbm, base, load_sem.at[2]),
        pltpu.make_async_copy(rot_hbm, rot, load_sem.at[3]),
    ]
    for load in loads:
        load.start()

    barrier = pltpu.get_barrier_semaphore()

    def greet(r2, w2):
        pl.semaphore_signal(barrier, inc=1, device_id=(r2, w2), device_id_type=MESH)

    @pl.when(holder)
    def _():
        for dz, dy, dc in FAR:
            greet((((r >> 3) + dz) & 7) * 8 + (((r >> 1) + dy) & 3) * 2 + (core ^ dc), w)

    greet(other_core, w)
    greet(other_chip, w)
    for d in range(1, WINDOWS):
        greet(member(keeps), lax.bitwise_and(w + d, WINDOWS - 1))

    @pl.when(jnp.logical_not(own))
    def _():
        greet(member(keeps), w)

    loads[0].wait()
    for c in range(CHAN):
        both = spec[c]
        power = jnp.sum(both * both, axis=(0, 1), keepdims=True) / BINS
        scale = jnp.broadcast_to(lax.rsqrt(power + 1e-06), (2, 128))
        mark[c] = scale
        for j in range(2):
            chans[me, TILES, CHAN * j + c : CHAN * j + c + 1, :] = scale[0:1]
        for t in range(TILES):
            chans[me, t, c : c + 1, :] = both[0:1, 128 * t : 128 * t + 128]
            chans[me, t, CHAN + c : CHAN + c + 1, :] = both[1:2, 128 * t : 128 * t + 128]

    pl.semaphore_wait(barrier, ITEMS - holder.astype(jnp.int32) + WINDOWS - own.astype(jnp.int32) + 2)

    def tell(i, carry):
        t = jnp.int32(SPARE + i) if i < 2 else 16 * ((i - 2) // 16) + ((r + i) & 15)
        r2 = jnp.where(t < SPARE, t, t - SPARE + LATE)
        piece = spec.at[:, :, pl.ds(pl.multiple_of(t * 128, 128), 128)]

        @pl.when(r2 == r)
        def _():
            pltpu.make_async_copy(piece, heard.at[r], hear_recv).start()

        @pl.when(r2 != r)
        def _():
            pltpu.make_async_remote_copy(
                piece, heard.at[r], hear_send, hear_recv, device_id=(r2, w), device_id_type=MESH
            ).start()

        return carry

    for i in range(TILES):
        tell(i, 0)

    def share(q, r2, sem):
        return pltpu.make_async_remote_copy(
            chans.at[q], chans.at[q], share_send.at[sem], share_recv.at[sem], device_id=(r2, w), device_id_type=MESH
        )

    to_chip = share(me, other_chip, 0)
    to_core = share(me, other_core, 1)
    to_core_too = share(me ^ 1, other_core, 2)
    to_chip.start()
    to_core.start()

    @pl.when(r == MARKER)
    def _():
        pltpu.make_async_copy(mark, heard.at[r], hear_recv).start()

    @pl.when(r != MARKER)
    def _():
        pltpu.make_async_remote_copy(
            mark, heard.at[r], hear_send, hear_recv, device_id=(MARKER, w), device_id_type=MESH
        ).start()

    loads[2].wait()
    loads[3].wait()

    z = lax.shift_right_logical(r, 3)
    y = (r >> 1) & 3
    flip = jnp.where((z >= 2) & (z <= 5), 3, 0)

    def tile_at(p):
        i = p >> 1
        shift = 2 * (i & 7)
        plane = ((jnp.where(i < 8, NEAR_Z[0], NEAR_Z[1]) >> shift) & 3) ^ flip
        line = (y + ((jnp.where(i < 8, NEAR_Y[0], NEAR_Y[1]) >> shift) & 3)) & 3
        return jnp.where(p < SPARE, (plane << 3) + (line << 1) + (p & 1), p)

    def table(i, carry):
        p = lax.shift_right_logical(i, 3)
        u = tile_at(p)
        row = pl.multiple_of(lax.bitwise_and(i, 7) * 16, 16)
        ct = rot[u, 0:1, :]
        st = rot[u, 1:2, :]
        cb = base[pl.ds(row, 16), :]
        sb = base[pl.ds(row + 128, 16), :]
        place = pl.ds(pl.multiple_of(p * 128 + row, 16), 16)
        thi[0, place, :], tlo[0, place, :] = split(cb * ct - sb * st)
        thi[1, place, :], tlo[1, place, :] = split(sb * ct + cb * st)
        return carry

    lax.fori_loop(0, TILES * 8, table, 0)

    def mirrored(i, carry):
        row = pl.multiple_of(i * 16, 16)
        m = lax.broadcasted_iota(jnp.int32, (16, WIDE), 0) + row
        j = lax.broadcasted_iota(jnp.int32, (16, WIDE), 1)
        mirror[pl.ds(row, 16), :] = jnp.where((m + j == HALF) & (m > 0), 1.0, 0.0).astype(BF16)
        return carry

    lax.fori_loop(0, WIDE // 16, mirrored, 0)

    loads[1].wait()

    @pl.when(holder)
    def _():
        pltpu.make_async_copy(heard, heard, hear_recv).wait()
        for k in range(NSRC):
            s = src[k]
            pair = heard[lax.shift_right_logical(s, 2), lax.bitwise_and(s, 3)]
            v = k // 2
            q, place = min(v, WINDOWS - 1 - v), 2 * (v // TEAM) + k % 2
            picked[q, place : place + 1, :] = pair[0:1]
            picked[q, PART + place : PART + place + 1, :] = pair[1:2]
        pltpu.make_async_copy(picked.at[me], items.at[mine], item_recv.at[mine]).start()

        def spread(i, carry):
            r2 = i

            @pl.when(r2 != r)
            def _():
                pltpu.make_async_remote_copy(
                    picked.at[member_of(i)], items.at[mine], item_send, item_recv.at[mine], device_id=(r2, w), device_id_type=MESH
                ).start()

            return carry

        for i in ORDER:
            spread(i, 0)

    to_chip.wait()
    to_core_too.start()
    to_core.wait()
    to_core_too.wait()

    x = w >> 1
    near_x = ((me >> 1) - x) & 3
    far_x = (3 - (me >> 1) - x) & 3
    ahead = ((far_x == 2) | (near_x == 0)).astype(jnp.int32)
    upper = lax.broadcasted_iota(jnp.int32, (8, 128), 0) < CHAN

    def tile(p, carry):
        t = tile_at(p)
        taper = rot[t, 2:3, 0:128]
        col = pl.ds(pl.multiple_of(p * 128, 128), 128)
        for cc in range(TEAM):
            chan = chans[cc, t] * taper
            turned = pltpu.roll(chan, CHAN, 0)
            plus = jnp.where(upper, chan, -chan)
            pair = [
                items[t, k : k + 1, :] * plus + items[t, PART + k : PART + k + 1, :] * turned for k in range(PART)
            ]
            re, im = [], []
            for a, b in (pair[0:2], pair[2:4]):
                re.append(jnp.where(upper, a, pltpu.roll(b, CHAN, 0)))
                im.append(jnp.where(upper, pltpu.roll(a, CHAN, 0), b))
            at = 16 * cc
            for j, value in enumerate((re, im)):
                high, low = split(jnp.concatenate(value, axis=0))
                cross[j, at : at + 16, col] = high
                cross[j, 64 + at : 64 + at + 16, col] = low
        return carry

    def arrived(t):
        pltpu.make_async_copy(items.at[t], items.at[t], item_recv.at[t]).wait()

    for start, stop in GROUPS:
        for p in range(start, stop):
            arrived(tile_at(p))
        lax.fori_loop(start, stop, tile, 0)
        if stop == TILES:
            arrived(TILES)
        bins = slice(128 * start, 128 * stop)
        for n in range(4):
            j, cols = n % 2, slice(CUT * (n // 2), CUT * (n // 2) + CUT)
            both = jnp.dot(cross[j, :, bins], thi[j, bins, cols], preferred_element_type=F32)
            low = jnp.dot(cross[j, 0:64, bins], tlo[j, bins, cols], preferred_element_type=F32)
            value = both[0:64] + both[64:128] + low
            if start > 0:
                value = value + acc[n]
            if stop < TILES:
                acc[n] = value
                continue
            for g in range(8):
                cc, j = g // 2, g % 2
                scale = jnp.where(upper, items[TILES, 2 * j : 2 * j + 1, :], items[TILES, 2 * j + 1 : 2 * j + 2, :])
                scale = scale * chans[cc, TILES]
                part[n * 8 + g] = value[8 * g : 8 * g + 8] * jnp.concatenate([scale, scale], axis=1)
            for i in range(8):
                cc, j = me ^ (1, 3, 2, 0)[i % 4], ahead ^ (i // 4)
                r2, w2 = member(cc), jnp.where(j == 0, me, WINDOWS - 1 - me)
                g = n * 8 + cc * 2 + j
                self = (r2 == r) & (w2 == w)

                @pl.when(self)
                def _(n=n, g=g):
                    pltpu.make_async_copy(part.at[g], parts.at[n, w], part_recv.at[n]).start()

                @pl.when(jnp.logical_not(self))
                def _(n=n, g=g, r2=r2, w2=w2):
                    pltpu.make_async_remote_copy(
                        part.at[g], parts.at[n, w], part_send, part_recv.at[n], device_id=(r2, w2), device_id_type=MESH
                    ).start()

    total = []
    for n in range(4):
        pltpu.make_async_copy(parts.at[n], parts.at[n], part_recv.at[n]).wait()
        value = parts[n, 0]
        for v in range(1, WINDOWS):
            value = value + parts[n, v]
        total.append(value)
    even = jnp.concatenate(total[0::2], axis=1)
    odd = jnp.concatenate(total[1::2], axis=1)
    before = even + odd
    one = before.astype(BF16)
    rest = before - one.astype(F32)
    two = rest.astype(BF16)
    three = (rest - two.astype(F32)).astype(BF16)
    thrice = jnp.dot(jnp.concatenate([one, two, three], axis=0), mirror[...], preferred_element_type=F32)
    before = thrice[0:8] + thrice[8:16] + thrice[16:24]
    after = pltpu.roll(even - odd, HALF, 1)
    lane = lax.broadcasted_iota(jnp.int32, (8, WIDE), 1)
    left = jnp.where(lane < HALF, before, after)
    for k in range(2):
        out[k, :, 0:WIDE] = left[CHAN * k : CHAN * k + CHAN]
        out[k, :, WIDE:LAGS] = after[CHAN * k : CHAN * k + CHAN, 0 : LAGS - WIDE]

    @pl.when(holder)
    def _():
        pltpu.make_async_copy(heard.at[pl.ds(0, ITEMS - 1)], heard.at[pl.ds(0, ITEMS - 1)], hear_send).wait()
        pltpu.make_async_copy(items.at[pl.ds(0, RECV - 1)], items.at[pl.ds(0, RECV - 1)], item_send).wait()

    @pl.when(jnp.logical_not(holder))
    def _():
        pltpu.make_async_copy(heard.at[pl.ds(0, ITEMS)], heard.at[pl.ds(0, ITEMS)], hear_send).wait()

    @pl.when(own)
    def _():
        pltpu.make_async_copy(part.at[pl.ds(0, 28)], part.at[pl.ds(0, 28)], part_send).wait()

    @pl.when(jnp.logical_not(own))
    def _():
        pltpu.make_async_copy(part, part, part_send).wait()


def shards(spectra, sources):
    base, rot = tables()
    anywhere = pl.BlockSpec(memory_space=pl.ANY)
    vmem = pltpu.VMEM
    dma = pltpu.SemaphoreType.DMA
    return pl.pallas_call(
        kernel,
        out_shape=pltpu.VMEM((NSRC // WINDOWS, CHAN, LAGS), F32),
        in_specs=[anywhere] * 4,
        out_specs=pl.BlockSpec(memory_space=vmem),
        scratch_shapes=[
            vmem((CHAN, 2, BINS), F32),
            pltpu.SMEM((NSRC,), jnp.int32),
            vmem((RECV, CHAN, 2, 128), F32),
            vmem((CHAN, 2, 128), F32),
            vmem((TEAM, 2 * PART, 128), F32),
            vmem((RECV, 2 * PART, 128), F32),
            vmem((TEAM, ITEMS, 8, 128), F32),
            vmem((256, WIDE), F32),
            vmem((TILES, 8, WIDE), F32),
            vmem((2, BINS, WIDE), BF16),
            vmem((2, BINS, WIDE), BF16),
            vmem((WIDE, WIDE), BF16),
            vmem((2, 128, BINS), BF16),
            vmem((4, 64, CUT), F32),
            vmem((32, 8, CUT), F32),
            vmem((4, WINDOWS, 8, CUT), F32),
            dma((4,)),
            dma,
            dma,
            dma((3,)),
            dma((3,)),
            dma,
            dma((ITEMS,)),
            dma,
            dma((4,)),
        ],
        compiler_params=pltpu.CompilerParams(
            collective_id=0, has_side_effects=True, vmem_limit_bytes=60 * 1024 * 1024
        ),
    )(spectra, sources, jnp.asarray(base), jnp.asarray(rot))


def solution(mesh):
    in_specs = (P("win", "recv", None, None), P())
    out_specs = P("win", "recv", None)
    return jax.shard_map(shards, mesh=mesh, in_specs=in_specs, out_specs=out_specs, check_vma=False)
```

```python
import math

import jax
import jax.numpy as jnp
import numpy as np
from jax import lax
from jax.experimental import pallas as pl
from jax.experimental.pallas import tpu as pltpu
from jax.sharding import PartitionSpec as P

BINS = 4352
NFFT = 16384
FIRST = 256
HALF = 500
LAGS = 2 * HALF + 1
NSRC = 16
WINDOWS = 8
CHAN = 4
ROWS = 4
RECV = 64
TILES = BINS // 128
ITEMS = TILES + 1
TEAM = 4
PART = NSRC // TEAM
WIDE = 512
CUT = 256
GROUPS = ((0, 12), (12, 20), (20, 28), (28, 34))
NEAR = sorted(((z, y) for z in range(4) for y in range(4)), key=lambda at: at[0] + 2 * min(at[1], 4 - at[1]))
NEAR_Z = [sum(NEAR[8 * h + i][0] << (2 * i) for i in range(8)) for h in range(2)]
NEAR_Y = [sum(NEAR[8 * h + i][1] << (2 * i) for i in range(8)) for h in range(2)]
FAR = sorted(
    ((z, y, c) for z in range(8) for y in range(ROWS) for c in range(2) if z or y or c),
    key=lambda at: -min(at[0], 8 - at[0]) - 2 * min(at[1], 4 - at[1]),
)
MARKER = 32
LATE = 56
URGENT_Z = (0, 0.3, 2, 2.3, 4, 4.3, 5, 5.3)
URGENT_Y = (-0.2, -0.1, 0.1, 0)
ORDER = sorted(range(RECV), key=lambda r2: URGENT_Z[r2 // 8] + URGENT_Y[r2 // 2 % 4])
SPARE = RECV // 2
MESH = pl.DeviceIdType.MESH
F32 = jnp.float32
BF16 = jnp.bfloat16


def tables():
    lags = np.arange(WIDE, dtype=np.int64)
    turn = 2.0 * np.pi / NFFT
    inner = (np.arange(128)[:, None] * lags[None, :]) % NFFT * turn
    base = np.concatenate([np.cos(inner), np.sin(inner)]).astype(np.float32)
    first = FIRST + 128 * np.arange(TILES, dtype=np.int64)
    outer = (first[:, None] * lags[None, :]) % NFFT * turn
    rot = np.zeros((TILES, 8, WIDE), np.float32)
    rot[:, 0] = np.cos(outer)
    rot[:, 1] = np.sin(outer)
    taper = np.sin(np.pi * (np.arange(BINS) + 0.5) / BINS) / math.sqrt(WINDOWS * BINS)
    rot[:, 2, :128] = taper.reshape(TILES, 128)
    return base, rot


def member_of(r):
    return (r & 1) * 2 + ((r >> 3) & 1)


def split(value):
    high = value.astype(BF16)
    return high, (value - high.astype(F32)).astype(BF16)


def kernel(
    spec_hbm, src_hbm, base_hbm, rot_hbm, out,
    spec, src, heard, mark, picked, items, chans, base, rot, thi, tlo, mirror, cross, acc, part, parts,
    load_sem, hear_send, hear_recv, share_send, share_recv, item_send, item_recv, part_send, part_recv,
):
    r = lax.axis_index("recv")
    w = lax.axis_index("win")
    core = lax.rem(r, 2)
    me = member_of(r)
    team = r - core - 8 * (me & 1)

    def member(q):
        return team + 8 * (q & 1) + (q >> 1)

    keeps = jnp.where(w < TEAM, w, WINDOWS - 1 - w)
    holder = (r < SPARE) | (r == MARKER) | (r == LATE) | (r == LATE + 1)
    mine = jnp.where(r < SPARE, r, jnp.where(r == MARKER, TILES, SPARE + r - LATE))
    own = me == keeps
    other_core = r + 1 - 2 * core
    other_chip = member(me ^ 1)

    loads = [
        pltpu.make_async_copy(spec_hbm.at[0], spec, load_sem.at[0]),
        pltpu.make_async_copy(src_hbm, src, load_sem.at[1]),
        pltpu.make_async_copy(base_hbm, base, load_sem.at[2]),
        pltpu.make_async_copy(rot_hbm, rot, load_sem.at[3]),
    ]
    for load in loads:
        load.start()

    barrier = pltpu.get_barrier_semaphore()

    def greet(r2, w2):
        pl.semaphore_signal(barrier, inc=1, device_id=(r2, w2), device_id_type=MESH)

    @pl.when(holder)
    def _():
        for dz, dy, dc in FAR:
            greet((((r >> 3) + dz) & 7) * 8 + (((r >> 1) + dy) & 3) * 2 + (core ^ dc), w)

    greet(other_core, w)
    greet(other_chip, w)
    for d in range(1, WINDOWS):
        greet(member(keeps), lax.bitwise_and(w + d, WINDOWS - 1))

    @pl.when(jnp.logical_not(own))
    def _():
        greet(member(keeps), w)

    loads[0].wait()
    for c in range(CHAN):
        both = spec[c]
        power = jnp.sum(both * both, axis=(0, 1), keepdims=True) / BINS
        scale = jnp.broadcast_to(lax.rsqrt(power + 1e-06), (2, 128))
        mark[c] = scale
        for j in range(2):
            chans[me, TILES, CHAN * j + c : CHAN * j + c + 1, :] = scale[0:1]
        for t in range(TILES):
            chans[me, t, c : c + 1, :] = both[0:1, 128 * t : 128 * t + 128]
            chans[me, t, CHAN + c : CHAN + c + 1, :] = both[1:2, 128 * t : 128 * t + 128]

    pl.semaphore_wait(barrier, ITEMS - holder.astype(jnp.int32) + WINDOWS - own.astype(jnp.int32) + 2)

    def tell(i, carry):
        t = jnp.int32(SPARE + i) if i < 2 else 16 * ((i - 2) // 16) + ((r + i) & 15)
        r2 = jnp.where(t < SPARE, t, t - SPARE + LATE)
        piece = spec.at[:, :, pl.ds(pl.multiple_of(t * 128, 128), 128)]

        @pl.when(r2 == r)
        def _():
            pltpu.make_async_copy(piece, heard.at[r], hear_recv).start()

        @pl.when(r2 != r)
        def _():
            pltpu.make_async_remote_copy(
                piece, heard.at[r], hear_send, hear_recv, device_id=(r2, w), device_id_type=MESH
            ).start()

        return carry

    for i in range(TILES):
        tell(i, 0)

    def share(q, r2, sem):
        return pltpu.make_async_remote_copy(
            chans.at[q], chans.at[q], share_send.at[sem], share_recv.at[sem], device_id=(r2, w), device_id_type=MESH
        )

    to_chip = share(me, other_chip, 0)
    to_core = share(me, other_core, 1)
    to_core_too = share(me ^ 1, other_core, 2)
    to_chip.start()
    to_core.start()

    @pl.when(r == MARKER)
    def _():
        pltpu.make_async_copy(mark, heard.at[r], hear_recv).start()

    @pl.when(r != MARKER)
    def _():
        pltpu.make_async_remote_copy(
            mark, heard.at[r], hear_send, hear_recv, device_id=(MARKER, w), device_id_type=MESH
        ).start()

    loads[2].wait()
    loads[3].wait()

    z = lax.shift_right_logical(r, 3)
    y = (r >> 1) & 3
    flip = jnp.where((z >= 2) & (z <= 5), 3, 0)

    def tile_at(p):
        i = p >> 1
        shift = 2 * (i & 7)
        plane = ((jnp.where(i < 8, NEAR_Z[0], NEAR_Z[1]) >> shift) & 3) ^ flip
        line = (y + ((jnp.where(i < 8, NEAR_Y[0], NEAR_Y[1]) >> shift) & 3)) & 3
        return jnp.where(p < SPARE, (plane << 3) + (line << 1) + (p & 1), p)

    def table(i, carry):
        p = lax.shift_right_logical(i, 3)
        u = tile_at(p)
        row = pl.multiple_of(lax.bitwise_and(i, 7) * 16, 16)
        ct = rot[u, 0:1, :]
        st = rot[u, 1:2, :]
        cb = base[pl.ds(row, 16), :]
        sb = base[pl.ds(row + 128, 16), :]
        place = pl.ds(pl.multiple_of(p * 128 + row, 16), 16)
        thi[0, place, :], tlo[0, place, :] = split(cb * ct - sb * st)
        thi[1, place, :], tlo[1, place, :] = split(sb * ct + cb * st)
        return carry

    lax.fori_loop(0, TILES * 8, table, 0)

    def mirrored(i, carry):
        row = pl.multiple_of(i * 16, 16)
        m = lax.broadcasted_iota(jnp.int32, (16, WIDE), 0) + row
        j = lax.broadcasted_iota(jnp.int32, (16, WIDE), 1)
        mirror[pl.ds(row, 16), :] = jnp.where((m + j == HALF) & (m > 0), 1.0, 0.0).astype(BF16)
        return carry

    lax.fori_loop(0, WIDE // 16, mirrored, 0)

    loads[1].wait()

    @pl.when(holder)
    def _():
        pltpu.make_async_copy(heard, heard, hear_recv).wait()
        for k in range(NSRC):
            s = src[k]
            pair = heard[lax.shift_right_logical(s, 2), lax.bitwise_and(s, 3)]
            v = k // 2
            q, place = min(v, WINDOWS - 1 - v), 2 * (v // TEAM) + k % 2
            picked[q, place : place + 1, :] = pair[0:1]
            picked[q, PART + place : PART + place + 1, :] = pair[1:2]
        pltpu.make_async_copy(picked.at[me], items.at[mine], item_recv.at[mine]).start()

        def spread(i, carry):
            r2 = i

            @pl.when(r2 != r)
            def _():
                pltpu.make_async_remote_copy(
                    picked.at[member_of(i)], items.at[mine], item_send, item_recv.at[mine], device_id=(r2, w), device_id_type=MESH
                ).start()

            return carry

        for i in ORDER:
            spread(i, 0)

    to_chip.wait()
    to_core_too.start()
    to_core.wait()
    to_core_too.wait()

    x = w >> 1
    near_x = ((me >> 1) - x) & 3
    far_x = (3 - (me >> 1) - x) & 3
    ahead = ((far_x == 2) | (near_x == 0)).astype(jnp.int32)
    upper = lax.broadcasted_iota(jnp.int32, (8, 128), 0) < CHAN

    def tile(p, carry):
        t = tile_at(p)
        taper = rot[t, 2:3, 0:128]
        col = pl.ds(pl.multiple_of(p * 128, 128), 128)
        for cc in range(TEAM):
            chan = chans[cc, t] * taper
            turned = pltpu.roll(chan, CHAN, 0)
            plus = jnp.where(upper, chan, -chan)
            pair = [
                items[t, k : k + 1, :] * plus + items[t, PART + k : PART + k + 1, :] * turned for k in range(PART)
            ]
            re, im = [], []
            for a, b in (pair[0:2], pair[2:4]):
                re.append(jnp.where(upper, a, pltpu.roll(b, CHAN, 0)))
                im.append(jnp.where(upper, pltpu.roll(a, CHAN, 0), b))
            at = 16 * cc
            for j, value in enumerate((re, im)):
                high, low = split(jnp.concatenate(value, axis=0))
                cross[j, at : at + 16, col] = high
                cross[j, 64 + at : 64 + at + 16, col] = low
        return carry

    def arrived(t):
        pltpu.make_async_copy(items.at[t], items.at[t], item_recv.at[t]).wait()

    for start, stop in GROUPS:
        for p in range(start, stop):
            arrived(tile_at(p))
        lax.fori_loop(start, stop, tile, 0)
        if stop == TILES:
            arrived(TILES)
        bins = slice(128 * start, 128 * stop)
        for n in range(4):
            j, cols = n % 2, slice(CUT * (n // 2), CUT * (n // 2) + CUT)
            both = jnp.dot(cross[j, :, bins], thi[j, bins, cols], preferred_element_type=F32)
            low = jnp.dot(cross[j, 0:64, bins], tlo[j, bins, cols], preferred_element_type=F32)
            value = both[0:64] + both[64:128] + low
            if start > 0:
                value = value + acc[n]
            if stop < TILES:
                acc[n] = value
                continue
            for g in range(8):
                cc, j = g // 2, g % 2
                scale = jnp.where(upper, items[TILES, 2 * j : 2 * j + 1, :], items[TILES, 2 * j + 1 : 2 * j + 2, :])
                scale = scale * chans[cc, TILES]
                part[n // 2 * 8 + g, :, CUT * (n % 2) : CUT * (n % 2) + CUT] = value[8 * g : 8 * g + 8] * jnp.concatenate(
                    [scale, scale], axis=1
                )
            if n % 2 == 0:
                continue
            h = n // 2
            for i in range(8):
                cc, j = me ^ (1, 3, 2, 0)[i % 4], ahead ^ (i // 4)
                r2, w2 = member(cc), jnp.where(j == 0, me, WINDOWS - 1 - me)
                g = h * 8 + cc * 2 + j
                self = (r2 == r) & (w2 == w)

                @pl.when(self)
                def _(h=h, g=g):
                    pltpu.make_async_copy(part.at[g], parts.at[h, w], part_recv.at[h]).start()

                @pl.when(jnp.logical_not(self))
                def _(h=h, g=g, r2=r2, w2=w2):
                    pltpu.make_async_remote_copy(
                        part.at[g], parts.at[h, w], part_send, part_recv.at[h], device_id=(r2, w2), device_id_type=MESH
                    ).start()

    total = []
    for h in range(2):
        pltpu.make_async_copy(parts.at[h], parts.at[h], part_recv.at[h]).wait()
        value = parts[h, 0]
        for v in range(1, WINDOWS):
            value = value + parts[h, v]
        total.append(value)
    even = jnp.concatenate([value[:, 0:CUT] for value in total], axis=1)
    odd = jnp.concatenate([value[:, CUT:] for value in total], axis=1)
    before = even + odd
    one = before.astype(BF16)
    rest = before - one.astype(F32)
    two = rest.astype(BF16)
    three = (rest - two.astype(F32)).astype(BF16)
    thrice = jnp.dot(jnp.concatenate([one, two, three], axis=0), mirror[...], preferred_element_type=F32)
    before = thrice[0:8] + thrice[8:16] + thrice[16:24]
    after = pltpu.roll(even - odd, HALF, 1)
    lane = lax.broadcasted_iota(jnp.int32, (8, WIDE), 1)
    left = jnp.where(lane < HALF, before, after)
    for k in range(2):
        out[k, :, 0:WIDE] = left[CHAN * k : CHAN * k + CHAN]
        out[k, :, WIDE:LAGS] = after[CHAN * k : CHAN * k + CHAN, 0 : LAGS - WIDE]

    @pl.when(holder)
    def _():
        pltpu.make_async_copy(heard.at[pl.ds(0, ITEMS - 1)], heard.at[pl.ds(0, ITEMS - 1)], hear_send).wait()
        pltpu.make_async_copy(items.at[pl.ds(0, RECV - 1)], items.at[pl.ds(0, RECV - 1)], item_send).wait()

    @pl.when(jnp.logical_not(holder))
    def _():
        pltpu.make_async_copy(heard.at[pl.ds(0, ITEMS)], heard.at[pl.ds(0, ITEMS)], hear_send).wait()

    @pl.when(own)
    def _():
        pltpu.make_async_copy(part.at[pl.ds(0, 14)], part.at[pl.ds(0, 14)], part_send).wait()

    @pl.when(jnp.logical_not(own))
    def _():
        pltpu.make_async_copy(part, part, part_send).wait()


def shards(spectra, sources):
    base, rot = tables()
    anywhere = pl.BlockSpec(memory_space=pl.ANY)
    vmem = pltpu.VMEM
    dma = pltpu.SemaphoreType.DMA
    return pl.pallas_call(
        kernel,
        out_shape=pltpu.VMEM((NSRC // WINDOWS, CHAN, LAGS), F32),
        in_specs=[anywhere] * 4,
        out_specs=pl.BlockSpec(memory_space=vmem),
        scratch_shapes=[
            vmem((CHAN, 2, BINS), F32),
            pltpu.SMEM((NSRC,), jnp.int32),
            vmem((RECV, CHAN, 2, 128), F32),
            vmem((CHAN, 2, 128), F32),
            vmem((TEAM, 2 * PART, 128), F32),
            vmem((RECV, 2 * PART, 128), F32),
            vmem((TEAM, ITEMS, 8, 128), F32),
            vmem((256, WIDE), F32),
            vmem((TILES, 8, WIDE), F32),
            vmem((2, BINS, WIDE), BF16),
            vmem((2, BINS, WIDE), BF16),
            vmem((WIDE, WIDE), BF16),
            vmem((2, 128, BINS), BF16),
            vmem((4, 64, CUT), F32),
            vmem((16, 8, 2 * CUT), F32),
            vmem((2, WINDOWS, 8, 2 * CUT), F32),
            dma((4,)),
            dma,
            dma,
            dma((3,)),
            dma((3,)),
            dma,
            dma((ITEMS,)),
            dma,
            dma((2,)),
        ],
        compiler_params=pltpu.CompilerParams(
            collective_id=0, has_side_effects=True, vmem_limit_bytes=60 * 1024 * 1024
        ),
    )(spectra, sources, jnp.asarray(base), jnp.asarray(rot))


def solution(mesh):
    in_specs = (P("win", "recv", None, None), P())
    out_specs = P("win", "recv", None)
    return jax.shard_map(shards, mesh=mesh, in_specs=in_specs, out_specs=out_specs, check_vma=False)
```
